128 devices in a mesh: group: 8 (over y, core), seq: 16 (over z, x).
Axes of the slice: x: 4, y: 4, z: 4, core: 2. Of those that a mesh axis runs over, the one named last changes fastest.
Arguments:
- q_nope: bfloat16 [32, 3, 128, 128], P('group', None, 'seq'), may hold values from -6 to 6
- q_rope: bfloat16 [32, 3, 128, 64], P('group', None, 'seq'), may hold values from -7 to 7
- w_absorb: bfloat16 [128, 128, 512], P('seq'), may hold values from -0.5 to 0.5
- w_value: bfloat16 [128, 512, 128], P('seq'), may hold values from -0.25 to 0.25
- cache: bfloat16 [16, 32768, 576], P('group', 'seq'), may hold values from -7 to 7
- res_len: int32 [16], P('group'), may hold values from 4096 to 32768
- prefill_rows: bfloat16 [8, 128, 128, 576], P('group', 'seq'), may hold values from -7 to 7
- block_dest: int32 [8, 128], P('group', 'seq'), may hold values from 0 to 15, as said below
- new_rows: bfloat16 [32, 3, 576], P('group'), may hold values from -7 to 7
Outputs:
- attention_out: bfloat16 [32, 3, 128, 128], P('group', None, 'seq')
The draws below stay inside these ranges and needn't reach their ends.
Inputs may be any that keep to these rules, and one draw needn't show every extreme that they name: `block_dest`: each prefill device sends at most 2 blocks to any one decode group (value // 2); for every index along seq one decode group gets exactly 2 blocks from the device of that index in every group, at least one for each of its new requests.
All inputs are finite; a program needn't handle non-finite values.
Results may differ from the reference program's by a relative error of at most 0.0081.
Values may be sent and summed in bfloat16 or wider, within the bound.
A program may use at most 192 MiB of HBM per device.

```python
import jax
import jax.numpy as jnp
from jax import lax

H = 128
NOPE = 128
ROPE = 64
LAT = 512
VDIM = 128
STEPS = 3
RES = 2
NEWD = 2
BATCH = 4
BLK = 128
NBD = 8
CAP = 2
CTX = 32768
REQS = 32
NEWREQ = 16
PBLOCKS = 128
N_GROUP = 8
N_SEQ = 16


def common_part(key):
    base = jax.random.normal(jax.random.fold_in(key, 501), (REQS, STEPS, ROPE), jnp.float32)
    return jnp.clip(base, -3.5, 3.5)


def block_owner(key):
    key = jax.random.fold_in(key, 503)
    hottest = jax.random.randint(jax.random.fold_in(key, 1), (N_SEQ,), 0, N_GROUP)

    def one_source(source):
        source_key = jax.random.fold_in(key, source + 2)
        hot_here = hottest[source % N_SEQ]
        spread = jax.random.permutation(jax.random.fold_in(source_key, 1), (N_GROUP - 1) * CAP)[:NBD - CAP] // CAP
        others = spread + (spread >= hot_here).astype(jnp.int32)
        groups = jnp.concatenate([jnp.full((CAP,), hot_here, jnp.int32), others.astype(jnp.int32)])
        member = jnp.concatenate([jnp.arange(CAP, dtype=jnp.int32) % NEWD, jax.random.randint(jax.random.fold_in(source_key, 2), (NBD - CAP,), 0, NEWD)])
        owner_ids = groups * NEWD + member
        shuffle = jax.random.permutation(jax.random.fold_in(source_key, 3), NBD)
        return owner_ids[shuffle]
    owners = jax.vmap(one_source)(jnp.arange(N_GROUP * N_SEQ, dtype=jnp.int32))
    return owners.reshape(N_GROUP, N_SEQ * NBD).astype(jnp.int32)


def draw_block_dest(key, part):
    return block_owner(key)


def draw_res_len(key, part):
    key = jax.random.fold_in(key, 11)
    number = N_GROUP * RES
    lengths = jax.random.randint(jax.random.fold_in(key, 1), (number,), CTX // 8, CTX + 1)
    shuffle = jax.random.permutation(jax.random.fold_in(key, 2), number)
    lengths = lengths.at[shuffle[0]].set(CTX).at[shuffle[1]].set(CTX // 8)
    return lengths.astype(jnp.int32)


def draw_q_rope(key, part):
    common = common_part(key)
    key = jax.random.fold_in(key, 12)
    noise = jax.random.normal(key, (REQS, STEPS, H, ROPE), jnp.float32)
    values = common[:, :, None, :] + noise
    return jnp.clip(values, -7.0, 7.0).astype(jnp.bfloat16)


def draw_cache(key, part):
    key = jax.random.fold_in(key, 13)
    number = N_GROUP * RES
    array_shape = (number, CTX, LAT + ROPE)
    values = jax.random.normal(key, array_shape, jnp.float32)
    return jnp.clip(values, -7.0, 7.0).astype(jnp.bfloat16)


def draw_prefill_rows(key, part):
    key = jax.random.fold_in(key, 14)
    array_shape = (N_GROUP, PBLOCKS, BLK, LAT + ROPE)
    values = jax.random.normal(key, array_shape, jnp.float32)
    return jnp.clip(values, -7.0, 7.0).astype(jnp.bfloat16)


def draw_new_rows(key, part):
    common = common_part(key)
    key = jax.random.fold_in(key, 15)
    latent = jax.random.normal(key, (REQS, STEPS, LAT), jnp.float32)
    values = jnp.concatenate([latent, 2.0 * common], axis=-1)
    return jnp.clip(values, -7.0, 7.0).astype(jnp.bfloat16)


def block_scale(own_key, shape, cuts, low, top_value):
    factor_of, own = 1.0, jax.random.fold_in(own_key, 6)
    for dim, shards_of in cuts:
        draws = jnp.exp(jax.random.uniform(jax.random.fold_in(own, dim), (shards_of,), jnp.float32, low / len(cuts), top_value / len(cuts)))
        factor_of = factor_of * jnp.repeat(draws, shape[dim] // shards_of).reshape([-1 if axis == dim else 1 for axis in range(len(shape))])
    return factor_of


def normal_values(rng, shape, scale, limit, cuts=(), held_as=jnp.bfloat16):
    result = scale * jax.random.normal(rng, shape, jnp.float32)
    if cuts:
        result = result * block_scale(rng, shape, cuts, -0.22, 0.18)
    return jnp.clip(result, -limit, limit).astype(held_as)


def setup_inputs(seed: int = 0) -> dict:
    arg_keys = jax.random.split(jax.random.key(seed), 10)
    q_nope = normal_values(arg_keys[0], (REQS, STEPS, H, NOPE), 1.0, 6.0, ((0, 8), (2, 16)))
    q_rope = draw_q_rope(jax.random.fold_in(arg_keys[9], 71), 0)
    w_absorb = normal_values(arg_keys[2], (H, NOPE, LAT), NOPE ** -0.5, 0.5, ((0, 16),))
    w_value = normal_values(arg_keys[3], (H, LAT, VDIM), LAT ** -0.5, 0.25, ((0, 16),))
    cache = draw_cache(jax.random.fold_in(arg_keys[9], 71), 0)
    res_len = draw_res_len(jax.random.fold_in(arg_keys[9], 71), 0)
    prefill_rows = draw_prefill_rows(jax.random.fold_in(arg_keys[9], 71), 0)
    block_dest = draw_block_dest(jax.random.fold_in(arg_keys[9], 71), 0)
    new_rows = draw_new_rows(jax.random.fold_in(arg_keys[9], 71), 0)
    return {"q_nope": q_nope, "q_rope": q_rope, "w_absorb": w_absorb, "w_value": w_value, "cache": cache, "res_len": res_len, "prefill_rows": prefill_rows, "block_dest": block_dest, "new_rows": new_rows}


masked_score = -1.0e30


def fresh_scores(query, fresh, scaling, causal_rows):
    scores = jnp.dot(query, fresh.T, preferred_element_type=jnp.float32) * scaling
    return jnp.where(causal_rows, scores, masked_score)


def reference(q_nope, q_rope, w_absorb, w_value, cache, res_len, prefill_rows, block_dest, new_rows):
    scaling = (NOPE + ROPE) ** -0.5
    row_width = LAT + ROPE
    q_latent = jnp.einsum("rthn,hnl->rthl", q_nope.astype(jnp.float32), w_absorb.astype(jnp.float32)).astype(jnp.bfloat16)
    query_all = jnp.concatenate([q_latent, q_rope], axis=-1).reshape(N_GROUP, BATCH, STEPS * H, row_width)
    fresh_all = new_rows.reshape(N_GROUP, BATCH, STEPS, row_width)
    causal = jnp.arange(STEPS)[:, None] >= jnp.arange(STEPS)[None, :]
    causal_rows = jnp.repeat(causal, H, axis=0)
    positions = jnp.arange(CTX, dtype=jnp.int32)

    def resident_one(inputs):
        query, key_rows, length, fresh = inputs
        scores = jnp.dot(query, key_rows.T, preferred_element_type=jnp.float32) * scaling
        usable = positions[None, :] < length
        scores = jnp.where(usable, scores, masked_score)
        scores_new = fresh_scores(query, fresh, scaling, causal_rows)
        peaks = jnp.maximum(jnp.max(scores, axis=1), jnp.max(scores_new, axis=1))
        weights = jnp.where(usable, jnp.exp(scores - peaks[:, None]), 0.0)
        weights_new = jnp.where(causal_rows, jnp.exp(scores_new - peaks[:, None]), 0.0)
        totals = jnp.sum(weights, axis=1) + jnp.sum(weights_new, axis=1)
        weighted = jnp.dot(weights.astype(jnp.bfloat16), key_rows[:, :LAT], preferred_element_type=jnp.float32)
        weighted = weighted + jnp.dot(weights_new.astype(jnp.bfloat16), fresh[:, :LAT], preferred_element_type=jnp.float32)
        return (weighted / totals[:, None]).astype(jnp.bfloat16)

    res_query = query_all[:, :RES].reshape(N_GROUP * RES, STEPS * H, row_width)
    res_fresh = fresh_all[:, :RES].reshape(N_GROUP * RES, STEPS, row_width)
    res_out = lax.map(resident_one, (res_query, cache, res_len, res_fresh))

    new_query = query_all[:, RES:].reshape(NEWREQ, STEPS * H, row_width)
    new_fresh = fresh_all[:, RES:].reshape(NEWREQ, STEPS, row_width)
    all_blocks = prefill_rows.reshape(N_GROUP * PBLOCKS, BLK, row_width)
    owners = block_dest.reshape(N_GROUP * PBLOCKS).astype(jnp.int32)

    def block_peak(inputs):
        row_block, owner_id = inputs
        query = lax.dynamic_index_in_dim(new_query, owner_id, 0, keepdims=False)
        return jnp.max(jnp.dot(query, row_block.T, preferred_element_type=jnp.float32) * scaling, axis=1)

    block_peaks = lax.map(block_peak, (all_blocks, owners))
    mine = owners[None, :] == jnp.arange(NEWREQ, dtype=jnp.int32)[:, None]
    scores_new = jax.vmap(lambda query, fresh: fresh_scores(query, fresh, scaling, causal_rows))(new_query, new_fresh)
    peaks = jnp.maximum(jnp.max(jnp.where(mine[:, :, None], block_peaks[None], masked_score), axis=1), jnp.max(scores_new, axis=2))

    def add_block(carry, inputs):
        weighted, totals = carry
        row_block, owner_id = inputs
        query = lax.dynamic_index_in_dim(new_query, owner_id, 0, keepdims=False)
        peak_row = lax.dynamic_index_in_dim(peaks, owner_id, 0, keepdims=False)
        scores = jnp.dot(query, row_block.T, preferred_element_type=jnp.float32) * scaling
        weights = jnp.exp(scores - peak_row[:, None])
        term = jnp.dot(weights.astype(jnp.bfloat16), row_block[:, :LAT], preferred_element_type=jnp.float32)
        weighted = lax.dynamic_update_index_in_dim(weighted, lax.dynamic_index_in_dim(weighted, owner_id, 0, keepdims=False) + term, owner_id, 0)
        totals = lax.dynamic_update_index_in_dim(totals, lax.dynamic_index_in_dim(totals, owner_id, 0, keepdims=False) + jnp.sum(weights, axis=1), owner_id, 0)
        return (weighted, totals), None

    initial = (jnp.zeros((NEWREQ, STEPS * H, LAT), jnp.float32), jnp.zeros((NEWREQ, STEPS * H), jnp.float32))
    (weighted, totals), unused = lax.scan(add_block, initial, (all_blocks, owners))
    weights_new = jnp.where(causal_rows[None], jnp.exp(scores_new - peaks[:, :, None]), 0.0)
    totals = totals + jnp.sum(weights_new, axis=2)
    rounded_new = lax.optimization_barrier(weights_new.astype(jnp.bfloat16))
    weighted = weighted + jnp.einsum("rms,rsl->rml", rounded_new.astype(jnp.float32), new_fresh[:, :, :LAT].astype(jnp.float32))
    new_out = (weighted / totals[:, :, None]).astype(jnp.bfloat16)

    attended = jnp.concatenate([res_out.reshape(N_GROUP, RES, STEPS, H, LAT), new_out.reshape(N_GROUP, NEWD, STEPS, H, LAT)], axis=1)
    attended = attended.reshape(REQS, STEPS, H, LAT)
    return jnp.einsum("rthl,hlv->rthv", attended.astype(jnp.float32), w_value.astype(jnp.float32)).astype(jnp.bfloat16)
```

```python
import math

import jax
import jax.numpy as jnp
from jax import lax
from jax.experimental import pallas as pl
from jax.experimental.pallas import tpu as pltpu
from jax.sharding import PartitionSpec as P

MESH = pl.DeviceIdType.MESH
F32 = jnp.float32
BF16 = jnp.bfloat16

NY, NC, NZ, NX = 4, 2, 4, 4
HEADS = 8
STEPS = 3
PART = STEPS * HEADS
ROWS = 2 * PART
NSEQ = NZ * NX
QROWS = NSEQ * PART
LAT, ROPE = 512, 64
BLK = 128
CTX = 2048
QMSG = 5 * ROWS
QCUT = 128
PMSG = 4 * ROWS + 16
KMSG = 8 * BLK + BLK + 16
NEG = -1e30
EXPC = (128 + 64) ** -0.5 * math.log2(math.e)

GROUP = [(0, 0), (0, 1), (1, 0), (1, 1), (3, 0), (3, 1), (2, 0), (2, 1)]


def dot_t(a, b):
    return lax.dot_general(a, b, (((1,), (1,)), ((), ())), preferred_element_type=F32)


def dot(a, b):
    return jnp.dot(a, b, preferred_element_type=F32)


def kernel(
    qn_ref, qr_ref, wa_hbm, wv_hbm, cache_hbm, len_ref, pre_hbm, dest_ref, new_ref,
    out_ref,
    wa, wv, cache, pre, ysend, kv, qbuf, qall, scores, weights, acc, peak, total,
    fresh, fresh_w, fresh_m, fresh_l, pout, pin,
    local_sem, y_ss, y_rs, a_ss, a_rs, f_ss, f_rs, p_ss, p_rs,
):
    g, s = lax.axis_index("group"), lax.axis_index("seq")
    y, c = lax.div(g, NC), lax.rem(g, NC)
    z, x = lax.div(s, NX), lax.rem(s, NX)

    def group_of(dy, dc):
        return lax.rem(y + dy, NY) * NC + lax.rem(c + dc, NC)

    def seq_dev(dz, dx):
        return (g, lax.rem(z + dz, NZ) * NX + lax.rem(x + dx, NX))

    loads = [
        pltpu.make_async_copy(src, dst, local_sem.at[i])
        for i, (src, dst) in enumerate(
            [(pre_hbm.at[0], pre), (wa_hbm, wa), (cache_hbm, cache), (wv_hbm, wv)]
        )
    ]
    for load in loads:
        load.start()

    barrier = pltpu.get_barrier_semaphore()
    for dy, dc in GROUP[1:]:
        pl.semaphore_signal(barrier, inc=1, device_id=(group_of(dy, dc), s), device_id_type=MESH)
    for j in range(1, NSEQ):
        pl.semaphore_signal(
            barrier, inc=1, device_id=seq_dev(j // NX, j % NX), device_id_type=MESH
        )

    owners = [dest_ref[0, k] for k in range(8)]
    targets = [lax.div(o, 2) for o in owners]
    members = [lax.rem(o, 2) for o in owners]
    loads[0].wait()
    tag_row = lax.broadcasted_iota(jnp.int32, (16, 128), 0)
    for i, (dy, dc) in enumerate(GROUP):
        wanted = group_of(dy, dc)
        first = second = jnp.int32(0)
        tag_first = tag_second = jnp.int32(2)
        for k in reversed(range(8)):
            match = targets[k] == wanted
            second = jnp.where(match, first, second)
            tag_second = jnp.where(match, tag_first, tag_second)
            first = jnp.where(match, k, first)
            tag_first = jnp.where(match, members[k], tag_first)
        to = kv if i == 0 else ysend
        for slot, index in enumerate((first, second)):
            for p in range(4):
                to[i, pl.ds(p * 2 * BLK + slot * BLK, BLK), :] = pre[
                    index, :, p * 128 : (p + 1) * 128
                ]
        to[i, pl.ds(8 * BLK, BLK), :] = jnp.concatenate(
            [pre[first, :, LAT : LAT + ROPE], pre[second, :, LAT : LAT + ROPE]], axis=1
        )
        tags = jnp.where(tag_row < 8, tag_first, tag_second)
        to[i, pl.ds(9 * BLK, 16), :] = tags.astype(F32).astype(BF16)

    loads[1].wait()
    row = lax.broadcasted_iota(jnp.int32, (2 * ROWS, 128), 0)
    own = qn_ref[...].astype(F32)
    spread = [jnp.where((row & 7) == h, own, 0.0).astype(BF16) for h in range(HEADS)]
    q_latent = dot(jnp.concatenate(spread, axis=1), wa[...].reshape(HEADS * 128, LAT))
    q_latent = q_latent.astype(BF16)
    q_rope = jnp.concatenate([qr_ref[...], jnp.zeros((2 * ROWS, 128 - ROPE), BF16)], axis=1)
    for pair in range(2):
        rows = slice(pair * ROWS, (pair + 1) * ROWS)
        for p in range(4):
            qbuf[pair, 0, 0, pl.ds(p * ROWS, ROWS), :] = q_latent[rows, p * 128 : (p + 1) * 128]
        qbuf[pair, 0, 0, pl.ds(4 * ROWS, ROWS), :] = q_rope[rows]

    pl.semaphore_wait(barrier, 7 + NSEQ - 1)

    def group_copy(i):
        dy, dc = GROUP[i]
        there = GROUP.index(((NY - dy) % NY, dc))
        return pltpu.make_async_remote_copy(
            src_ref=ysend.at[i], dst_ref=kv.at[there], send_sem=y_ss.at[i], recv_sem=y_rs.at[there],
            device_id=(group_of(dy, dc), s), device_id_type=MESH,
        )

    group_copies = [group_copy(i) for i in range(1, 8)]
    for copy in group_copies:
        copy.start()

    low, high = pl.ds(0, QCUT), pl.ds(QCUT, QMSG - QCUT)

    def own_copy(pair, index, dz, dx, rows):
        return pltpu.make_async_remote_copy(
            src_ref=qbuf.at[pair, 0, 0, rows], dst_ref=qbuf.at[pair, (NZ - dz) % NZ, (NX - dx) % NX, rows],
            send_sem=a_ss.at[pair, index], recv_sem=a_rs.at[pair, index],
            device_id=seq_dev(dz, dx), device_id_type=MESH,
        )

    def x_first(pair):
        return [own_copy(pair, d - 1, 0, d, low) for d in (1, 2, 3)]

    def z_first(pair):
        return [own_copy(pair, 2 + d, d, 0, high) for d in (1, 2, 3)]

    def rest(pair):
        return [own_copy(pair, 5 + d, 0, d, high) for d in (1, 2, 3)] + [
            own_copy(pair, 8 + d, d, 0, low) for d in (1, 2, 3)
        ]

    def forward_z(pair):
        return [
            pltpu.make_async_remote_copy(
                src_ref=qbuf.at[pair, 0, pl.ds(1, 3), low], dst_ref=qbuf.at[pair, NZ - d, pl.ds(1, 3), low],
                send_sem=f_ss.at[pair, d - 1], recv_sem=f_rs.at[pair, d - 1],
                device_id=seq_dev(d, 0), device_id_type=MESH,
            )
            for d in (1, 2, 3)
        ]

    def forward_x(pair):
        return [
            pltpu.make_async_remote_copy(
                src_ref=qbuf.at[pair, pl.ds(1, 3), 0, high], dst_ref=qbuf.at[pair, pl.ds(1, 3), NX - d, high],
                send_sem=f_ss.at[pair, 2 + d], recv_sem=f_rs.at[pair, 2 + d],
                device_id=seq_dev(0, d), device_id_type=MESH,
            )
            for d in (1, 2, 3)
        ]

    def start(copies):
        for copy in copies:
            copy.start()
        return copies

    def arrived(copies):
        for copy in copies:
            copy.wait_recv()

    sent = []
    first_x, first_z = start(x_first(0)), start(z_first(0))
    others = start(rest(0))
    sent += first_x + first_z + others

    fresh[...] = jnp.zeros_like(fresh)
    for r in range(4):
        fresh[pl.ds(8 * r, STEPS), :] = new_ref[r].astype(F32)
    fresh_rows = fresh[...].astype(BF16)
    s_fresh = dot_t(q_latent, fresh_rows[:, :LAT]) + dot_t(
        qr_ref[...], fresh_rows[:, LAT : LAT + ROPE]
    )
    part = lax.broadcasted_iota(jnp.int32, (2 * ROWS, 32), 0) >> 3
    key = lax.broadcasted_iota(jnp.int32, (2 * ROWS, 32), 1)
    request = (
        (part >= 3).astype(jnp.int32) + (part >= 6).astype(jnp.int32) + (part >= 9).astype(jnp.int32)
    )
    step = part - 3 * request
    allowed = ((key >> 3) == request) & ((key & 7) <= step)
    s_fresh = jnp.where(allowed, s_fresh, NEG)
    m_fresh = jnp.max(s_fresh, axis=1, keepdims=True)
    p_fresh = jnp.where(allowed, jnp.exp2((s_fresh - m_fresh) * EXPC), 0.0)
    fresh_m[...] = jnp.broadcast_to(m_fresh, fresh_m.shape)
    fresh_l[...] = jnp.broadcast_to(jnp.sum(p_fresh, axis=1, keepdims=True), fresh_l.shape)
    fresh_w[...] = dot(p_fresh.astype(BF16), fresh_rows[:, :LAT])

    arrived(first_x)
    sent += (forward_z0 := start(forward_z(0)))
    arrived(first_z)
    sent += (forward_x0 := start(forward_x(0)))
    first_x1, first_z1 = start(x_first(1)), start(z_first(1))
    others1 = start(rest(1))
    sent += first_x1 + first_z1 + others1
    arrived(first_x1)
    sent += (forward_z1 := start(forward_z(1)))
    arrived(first_z1)
    sent += (forward_x1 := start(forward_x(1)))

    def assemble(pair):
        def two(i, carry):
            at = pl.multiple_of(i * 2 * PART, 16)
            dz, dx = lax.div(i, 2), lax.rem(i, 2) * 2
            for p in range(5):
                one = qbuf[pair, dz, dx, pl.ds(p * ROWS, ROWS), :].astype(F32)
                two = qbuf[pair, dz, dx + 1, pl.ds(p * ROWS, ROWS), :].astype(F32)
                lanes = slice(p * 128, (p + 1) * 128)
                for r in range(2):
                    rows = slice(r * PART, (r + 1) * PART)
                    qall[2 * pair + r, pl.ds(at, 2 * PART), lanes] = jnp.concatenate(
                        [one[rows], two[rows]], axis=0
                    ).astype(BF16)
            return carry

        lax.fori_loop(0, NSEQ // 2, two, 0)

    def pack(pair):
        lane = lax.broadcasted_iota(jnp.int32, (16, 128), 1)

        def one(j, carry):
            at = pl.multiple_of(j * PART, 8)

            def both(ref):
                return jnp.concatenate(
                    [ref[2 * pair, pl.ds(at, PART), :], ref[2 * pair + 1, pl.ds(at, PART), :]], axis=0
                )

            for p in range(4):
                lanes = slice(p * 128, (p + 1) * 128)
                pout[pair, j, pl.ds(p * ROWS, ROWS), :] = jnp.concatenate(
                    [acc[2 * pair, pl.ds(at, PART), lanes], acc[2 * pair + 1, pl.ds(at, PART), lanes]],
                    axis=0,
                ).astype(BF16)
            m, l = both(peak), both(total)
            m_high = m.astype(BF16).astype(F32)
            m_mid = (m - m_high).astype(BF16).astype(F32)
            m_low = m - m_high - m_mid
            l_high = l.astype(BF16).astype(F32)
            stats = jnp.zeros((16, 128), F32)
            for i in range(3):
                rows = slice(16 * i, 16 * (i + 1))
                for q, value in enumerate((m_high, m_mid, m_low, l_high, l - l_high)):
                    stats = jnp.where(lane == 8 * i + q, value[rows], stats)
            pout[pair, j, pl.ds(4 * ROWS, 16), :] = stats.astype(BF16)
            return carry

        lax.fori_loop(0, NSEQ, one, 0)

    def partial_copies(pair):
        return [
            pltpu.make_async_remote_copy(
                src_ref=pout.at[pair, j], dst_ref=pin.at[pair, (NZ - j // NX) % NZ * NX + (NX - j % NX) % NX],
                send_sem=p_ss.at[pair, j], recv_sem=p_rs.at[pair, j],
                device_id=seq_dev(j // NX, j % NX), device_id_type=MESH,
            )
            for j in range(1, NSEQ)
        ]

    def finish(pair):
        stats = jnp.concatenate(
            [pout[pair, 0, pl.ds(4 * ROWS, 16), :]]
            + [pin[pair, j, pl.ds(4 * ROWS, 16), :] for j in range(1, NSEQ)],
            axis=0,
        )
        source = lax.broadcasted_iota(jnp.int32, (128, 128), 0)
        picks = [
            ((source >= 8 * i) & (source < 8 * i + 3)).astype(F32).astype(BF16) for i in range(3)
        ] + [
            ((source >= 8 * i + 3) & (source < 8 * i + 5)).astype(F32).astype(BF16) for i in range(3)
        ]
        spread_stats = dot(stats, jnp.concatenate(picks, axis=1))

        def of(j, kind):
            return jnp.concatenate(
                [
                    spread_stats[16 * j : 16 * (j + 1), 128 * (3 * kind + i) : 128 * (3 * kind + i + 1)]
                    for i in range(3)
                ],
                axis=0,
            )

        rows = pl.ds(pair * ROWS, ROWS)
        peaks = [of(j, 0) for j in range(NSEQ)]
        m_fresh = fresh_m[rows, :]
        top = m_fresh
        for m in peaks:
            top = jnp.maximum(top, m)
        keep = jnp.exp2((m_fresh - top) * EXPC)
        sums = keep * fresh_l[rows, :]
        values = [keep * fresh_w[rows, p * 128 : (p + 1) * 128] for p in range(4)]
        for j in range(NSEQ):
            keep = jnp.exp2((peaks[j] - top) * EXPC)
            sums = sums + keep * of(j, 1)
            message = pout if j == 0 else pin
            for p in range(4):
                values[p] = values[p] + keep * message[pair, j, pl.ds(p * ROWS, ROWS), :].astype(F32)
        head = lax.broadcasted_iota(jnp.int32, (ROWS, 128), 0) & 7
        attended = [(v / sums).astype(BF16).astype(F32) for v in values]
        spread = [
            jnp.where(head == h, attended[p], 0.0).astype(BF16) for h in range(HEADS) for p in range(4)
        ]
        result = dot(jnp.concatenate(spread, axis=1), wv[...].reshape(HEADS * LAT, 128))
        out_ref[rows, :] = result.astype(BF16)

    arrived(others + forward_z0 + forward_x0)
    assemble(0)
    loads[2].wait()

    def resident(r, carry):
        limit = len_ref[r] - s * CTX
        tile = 512
        position = lax.broadcasted_iota(jnp.int32, (QROWS, tile), 1)
        running = jnp.full((QROWS, 128), NEG, F32)
        for k in range(CTX // tile):
            keys = pl.ds(k * tile, tile)
            sc = dot_t(qall[r, :, :LAT], cache[r, keys, :LAT]) + dot_t(
                qall[r, :, LAT : LAT + ROPE], cache[r, keys, LAT : LAT + ROPE]
            )
            sc = jnp.where(position < limit - k * tile, sc, NEG)
            scores[:, keys] = sc
            for i in range(tile // 128):
                running = jnp.maximum(running, sc[:, i * 128 : (i + 1) * 128])
        m = jnp.max(running, axis=1, keepdims=True)
        sums = jnp.zeros((QROWS, 128), F32)
        for k in range(CTX // tile):
            keys = pl.ds(k * tile, tile)
            w = jnp.exp2((scores[:, keys] - m) * EXPC)
            for i in range(tile // 128):
                sums = sums + w[:, i * 128 : (i + 1) * 128]
            weights[:, keys] = w.astype(BF16)
        acc[r] = dot(weights[...], cache[r, :, :LAT])
        peak[r] = jnp.broadcast_to(m, (QROWS, 128))
        total[r] = jnp.broadcast_to(jnp.sum(sums, axis=1, keepdims=True), (QROWS, 128))
        return carry

    lax.fori_loop(0, 2, resident, 0)
    pack(0)
    partials0 = start(partial_copies(0))

    arrived(others1 + forward_z1 + forward_x1)
    assemble(1)
    for r in (2, 3):
        acc[r] = jnp.zeros((QROWS, LAT), F32)
        peak[r] = jnp.full((QROWS, 128), NEG, F32)
        total[r] = jnp.zeros((QROWS, 128), F32)

    def blocks(i):
        latent = jnp.concatenate(
            [kv[i, pl.ds(p * 2 * BLK, 2 * BLK), :] for p in range(4)], axis=1
        )
        ropes = kv[i, pl.ds(8 * BLK, BLK), :]
        tags = kv[i, pl.ds(9 * BLK, 16), :].astype(F32)
        tag = jnp.concatenate([tags[0:1, :], tags[8:9, :]], axis=1)
        for r in (2, 3):
            q_rope = qall[r, :, LAT : LAT + ROPE]
            sc = dot_t(qall[r, :, :LAT], latent) + jnp.concatenate(
                [dot_t(q_rope, ropes[:, :ROPE]), dot_t(q_rope, ropes[:, ROPE:])], axis=1
            )
            sc = jnp.where(tag == float(r - 2), sc, NEG)
            old = peak[r]
            best = jnp.max(
                jnp.maximum(sc[:, :128], sc[:, 128:]), axis=1, keepdims=True
            )
            top = jnp.maximum(old, best)
            keep = jnp.exp2((old - top) * EXPC)
            w0 = jnp.exp2((sc[:, :128] - top) * EXPC)
            w1 = jnp.exp2((sc[:, 128:] - top) * EXPC)
            peak[r] = top
            total[r] = total[r] * keep + jnp.sum(w0 + w1, axis=1, keepdims=True)
            w = jnp.concatenate([w0, w1], axis=1).astype(BF16)
            term = dot(w, latent)
            for p in range(4):
                lanes = slice(p * 128, (p + 1) * 128)
                acc[r, :, lanes] = acc[r, :, lanes] * keep + term[:, lanes]

    def landed(i, carry):
        pltpu.make_async_remote_copy(
            src_ref=ysend.at[i], dst_ref=kv.at[i], send_sem=y_ss.at[i], recv_sem=y_rs.at[i],
            device_id=(group_of(0, 1), s), device_id_type=MESH,
        ).wait_recv()
        blocks(i)
        return carry

    blocks(0)
    lax.fori_loop(1, 6, landed, 0)
    loads[3].wait()
    arrived(partials0)
    finish(0)
    lax.fori_loop(6, 8, landed, 0)
    pack(1)
    partials1 = start(partial_copies(1))
    arrived(partials1)
    finish(1)
    for copy in group_copies + sent + partials0 + partials1:
        copy.wait_send()


def body(q_nope, q_rope, w_absorb, w_value, cache, res_len, prefill_rows, block_dest, new_rows):
    rows = 4 * PART
    vmem, hbm, smem = (
        pl.BlockSpec(memory_space=pltpu.VMEM),
        pl.BlockSpec(memory_space=pl.ANY),
        pl.BlockSpec(memory_space=pltpu.SMEM),
    )
    out = pl.pallas_call(
        kernel,
        out_shape=jax.ShapeDtypeStruct((rows, 128), BF16),
        in_specs=[vmem, vmem, hbm, hbm, hbm, smem, hbm, smem, vmem],
        out_specs=vmem,
        scratch_shapes=[
            pltpu.VMEM(w_absorb.shape, BF16),
            pltpu.VMEM(w_value.shape, BF16),
            pltpu.VMEM(cache.shape, BF16),
            pltpu.VMEM(prefill_rows.shape[1:], BF16),
            pltpu.VMEM((8, KMSG, 128), BF16),
            pltpu.VMEM((8, KMSG, 128), BF16),
            pltpu.VMEM((2, NZ, NX, QMSG, 128), BF16),
            pltpu.VMEM((4, QROWS, LAT + 128), BF16),
            pltpu.VMEM((QROWS, CTX), F32),
            pltpu.VMEM((QROWS, CTX), BF16),
            pltpu.VMEM((4, QROWS, LAT), F32),
            pltpu.VMEM((4, QROWS, 128), F32),
            pltpu.VMEM((4, QROWS, 128), F32),
            pltpu.VMEM((32, LAT + ROPE), F32),
            pltpu.VMEM((rows, LAT), F32),
            pltpu.VMEM((rows, 128), F32),
            pltpu.VMEM((rows, 128), F32),
            pltpu.VMEM((2, NSEQ, PMSG, 128), BF16),
            pltpu.VMEM((2, NSEQ, PMSG, 128), BF16),
            pltpu.SemaphoreType.DMA((4,)),
            pltpu.SemaphoreType.DMA((8,)),
            pltpu.SemaphoreType.DMA((8,)),
            pltpu.SemaphoreType.DMA((2, 12)),
            pltpu.SemaphoreType.DMA((2, 12)),
            pltpu.SemaphoreType.DMA((2, 6)),
            pltpu.SemaphoreType.DMA((2, 6)),
            pltpu.SemaphoreType.DMA((2, NSEQ)),
            pltpu.SemaphoreType.DMA((2, NSEQ)),
        ],
        compiler_params=pltpu.CompilerParams(
            collective_id=0, has_side_effects=True, vmem_limit_bytes=56 * 1024 * 1024
        ),
        name="latent_attention",
    )(
        q_nope.reshape(rows, 128),
        q_rope.reshape(rows, ROPE),
        w_absorb,
        w_value,
        cache,
        res_len,
        prefill_rows,
        block_dest,
        new_rows,
    )
    return out.reshape(q_nope.shape)


def solution(mesh):
    in_specs = (
        P("group", None, "seq", None),
        P("group", None, "seq", None),
        P("seq", None, None),
        P("seq", None, None),
        P("group", "seq", None),
        P("group"),
        P("group", "seq", None, None),
        P("group", "seq"),
        P("group", None, None),
    )
    out_specs = P("group", None, "seq", None)
    return jax.shard_map(body, mesh=mesh, in_specs=in_specs, out_specs=out_specs, check_vma=False)
```

```python
import math

import jax
import jax.numpy as jnp
from jax import lax
from jax.experimental import pallas as pl
from jax.experimental.pallas import tpu as pltpu
from jax.sharding import PartitionSpec as P

MESH = pl.DeviceIdType.MESH
F32 = jnp.float32
BF16 = jnp.bfloat16

NY, NC, NZ, NX = 4, 2, 4, 4
HEADS = 8
STEPS = 3
PART = STEPS * HEADS
ROWS = 2 * PART
NSEQ = NZ * NX
QROWS = NSEQ * PART
LAT, ROPE = 512, 64
BLK = 128
CTX = 2048
QMSG = 5 * ROWS
QCUT = 128
PMSG = 4 * ROWS + 16
ROW = LAT + ROPE
KMSG = 2 * ROW + 16
NEG = -1e30
EXPC = (128 + 64) ** -0.5 * math.log2(math.e)

GROUP = [(0, 0), (0, 1), (1, 0), (1, 1), (3, 0), (3, 1), (2, 0), (2, 1)]


def dot_t(a, b):
    return lax.dot_general(a, b, (((1,), (1,)), ((), ())), preferred_element_type=F32)


def dot(a, b):
    return jnp.dot(a, b, preferred_element_type=F32)


def kernel(
    qn_ref, qr_ref, wa_hbm, wv_hbm, cache_hbm, len_ref, pre_hbm, dest_ref, new_ref,
    out_ref,
    wa, wv, cache, pre, ysend, kv, qbuf, qall, scores, weights, acc, peak, total,
    fresh, fresh_w, fresh_m, fresh_l, pout, pin,
    local_sem, y_ss, y_rs, a_ss, a_rs, f_ss, f_rs, p_ss, p_rs,
):
    g, s = lax.axis_index("group"), lax.axis_index("seq")
    y, c = lax.div(g, NC), lax.rem(g, NC)
    z, x = lax.div(s, NX), lax.rem(s, NX)

    def group_of(dy, dc):
        return lax.rem(y + dy, NY) * NC + lax.rem(c + dc, NC)

    def seq_dev(dz, dx):
        return (g, lax.rem(z + dz, NZ) * NX + lax.rem(x + dx, NX))

    loads = [
        pltpu.make_async_copy(src, dst, local_sem.at[i])
        for i, (src, dst) in enumerate(
            [(pre_hbm.at[0], pre), (wa_hbm, wa), (cache_hbm, cache), (wv_hbm, wv)]
        )
    ]
    for load in loads:
        load.start()

    barrier = pltpu.get_barrier_semaphore()
    for dy, dc in GROUP[1:]:
        pl.semaphore_signal(barrier, inc=1, device_id=(group_of(dy, dc), s), device_id_type=MESH)
    for j in range(1, NSEQ):
        pl.semaphore_signal(
            barrier, inc=1, device_id=seq_dev(j // NX, j % NX), device_id_type=MESH
        )

    owners = [dest_ref[0, k] for k in range(8)]
    targets = [lax.div(o, 2) for o in owners]
    members = [lax.rem(o, 2) for o in owners]
    loads[0].wait()
    tag_row = lax.broadcasted_iota(jnp.int32, (16, 128), 0)
    for i, (dy, dc) in enumerate(GROUP):
        wanted = group_of(dy, dc)
        first = second = jnp.int32(0)
        tag_first = tag_second = jnp.int32(2)
        for k in reversed(range(8)):
            match = targets[k] == wanted
            second = jnp.where(match, first, second)
            tag_second = jnp.where(match, tag_first, tag_second)
            first = jnp.where(match, k, first)
            tag_first = jnp.where(match, members[k], tag_first)
        to = kv if i == 0 else ysend
        for slot, index in enumerate((first, second)):
            to[i, pl.ds(slot * ROW, ROW), :] = pre[index]
        tags = jnp.where(tag_row < 8, tag_first, tag_second)
        to[i, pl.ds(2 * ROW, 16), :] = tags.astype(F32).astype(BF16)

    loads[1].wait()
    row = lax.broadcasted_iota(jnp.int32, (2 * ROWS, 128), 0)
    own = qn_ref[...].astype(F32)
    spread = [jnp.where((row & 7) == h, own, 0.0).astype(BF16) for h in range(HEADS)]
    q_latent = dot(jnp.concatenate(spread, axis=1), wa[...].reshape(HEADS * 128, LAT))
    q_latent = q_latent.astype(BF16)
    q_rope = jnp.concatenate([qr_ref[...], jnp.zeros((2 * ROWS, 128 - ROPE), BF16)], axis=1)
    for pair in range(2):
        rows = slice(pair * ROWS, (pair + 1) * ROWS)
        for p in range(4):
            qbuf[pair, 0, 0, pl.ds(p * ROWS, ROWS), :] = q_latent[rows, p * 128 : (p + 1) * 128]
        qbuf[pair, 0, 0, pl.ds(4 * ROWS, ROWS), :] = q_rope[rows]

    pl.semaphore_wait(barrier, 7 + NSEQ - 1)

    def group_copy(i):
        dy, dc = GROUP[i]
        there = GROUP.index(((NY - dy) % NY, dc))
        return pltpu.make_async_remote_copy(
            src_ref=ysend.at[i], dst_ref=kv.at[there], send_sem=y_ss.at[i], recv_sem=y_rs.at[there],
            device_id=(group_of(dy, dc), s), device_id_type=MESH,
        )

    group_copies = [group_copy(i) for i in range(1, 8)]
    for copy in group_copies:
        copy.start()

    low, high = pl.ds(0, QCUT), pl.ds(QCUT, QMSG - QCUT)

    def own_copy(pair, index, dz, dx, rows):
        return pltpu.make_async_remote_copy(
            src_ref=qbuf.at[pair, 0, 0, rows], dst_ref=qbuf.at[pair, (NZ - dz) % NZ, (NX - dx) % NX, rows],
            send_sem=a_ss.at[pair, index], recv_sem=a_rs.at[pair, index],
            device_id=seq_dev(dz, dx), device_id_type=MESH,
        )

    def x_first(pair):
        return [own_copy(pair, d - 1, 0, d, low) for d in (1, 2, 3)]

    def z_first(pair):
        return [own_copy(pair, 2 + d, d, 0, high) for d in (1, 2, 3)]

    def rest(pair):
        return [own_copy(pair, 5 + d, 0, d, high) for d in (1, 2, 3)] + [
            own_copy(pair, 8 + d, d, 0, low) for d in (1, 2, 3)
        ]

    def forward_z(pair):
        return [
            pltpu.make_async_remote_copy(
                src_ref=qbuf.at[pair, 0, pl.ds(1, 3), low], dst_ref=qbuf.at[pair, NZ - d, pl.ds(1, 3), low],
                send_sem=f_ss.at[pair, d - 1], recv_sem=f_rs.at[pair, d - 1],
                device_id=seq_dev(d, 0), device_id_type=MESH,
            )
            for d in (1, 2, 3)
        ]

    def forward_x(pair):
        return [
            pltpu.make_async_remote_copy(
                src_ref=qbuf.at[pair, pl.ds(1, 3), 0, high], dst_ref=qbuf.at[pair, pl.ds(1, 3), NX - d, high],
                send_sem=f_ss.at[pair, 2 + d], recv_sem=f_rs.at[pair, 2 + d],
                device_id=seq_dev(0, d), device_id_type=MESH,
            )
            for d in (1, 2, 3)
        ]

    def start(copies):
        for copy in copies:
            copy.start()
        return copies

    def arrived(copies):
        for copy in copies:
            copy.wait_recv()

    sent = []
    first_x, first_z = start(x_first(0)), start(z_first(0))
    others = start(rest(0))
    sent += first_x + first_z + others

    fresh[...] = jnp.zeros_like(fresh)
    for u in range(STEPS):
        new = new_ref[u].astype(F32)
        for r in range(4):
            fresh[pl.ds(8 * r + u, 1), :] = new[r : r + 1]
    fresh_rows = fresh[...].astype(BF16)
    s_fresh = dot_t(q_latent, fresh_rows[:, :LAT]) + dot_t(
        qr_ref[...], fresh_rows[:, LAT : LAT + ROPE]
    )
    part = lax.broadcasted_iota(jnp.int32, (2 * ROWS, 32), 0) >> 3
    key = lax.broadcasted_iota(jnp.int32, (2 * ROWS, 32), 1)
    request = (
        (part >= 3).astype(jnp.int32) + (part >= 6).astype(jnp.int32) + (part >= 9).astype(jnp.int32)
    )
    step = part - 3 * request
    allowed = ((key >> 3) == request) & ((key & 7) <= step)
    s_fresh = jnp.where(allowed, s_fresh, NEG)
    m_fresh = jnp.max(s_fresh, axis=1, keepdims=True)
    p_fresh = jnp.where(allowed, jnp.exp2((s_fresh - m_fresh) * EXPC), 0.0)
    fresh_m[...] = jnp.broadcast_to(m_fresh, fresh_m.shape)
    fresh_l[...] = jnp.broadcast_to(jnp.sum(p_fresh, axis=1, keepdims=True), fresh_l.shape)
    fresh_w[...] = dot(p_fresh.astype(BF16), fresh_rows[:, :LAT])

    arrived(first_x)
    sent += (forward_z0 := start(forward_z(0)))
    arrived(first_z)
    sent += (forward_x0 := start(forward_x(0)))
    first_x1, first_z1 = start(x_first(1)), start(z_first(1))
    others1 = start(rest(1))
    sent += first_x1 + first_z1 + others1
    arrived(first_x1)
    sent += (forward_z1 := start(forward_z(1)))
    arrived(first_z1)
    sent += (forward_x1 := start(forward_x(1)))

    def assemble(pair):
        def two(i, carry):
            at = pl.multiple_of(i * 2 * PART, 16)
            dz, dx = lax.div(i, 2), lax.rem(i, 2) * 2
            for p in range(5):
                one = qbuf[pair, dz, dx, pl.ds(p * ROWS, ROWS), :].astype(F32)
                two = qbuf[pair, dz, dx + 1, pl.ds(p * ROWS, ROWS), :].astype(F32)
                lanes = slice(p * 128, (p + 1) * 128)
                for r in range(2):
                    rows = slice(r * PART, (r + 1) * PART)
                    qall[2 * pair + r, pl.ds(at, 2 * PART), lanes] = jnp.concatenate(
                        [one[rows], two[rows]], axis=0
                    ).astype(BF16)
            return carry

        lax.fori_loop(0, NSEQ // 2, two, 0)

    def pack(pair):
        lane = lax.broadcasted_iota(jnp.int32, (16, 128), 1)

        def one(j, carry):
            at = pl.multiple_of(j * PART, 8)

            def both(ref):
                return jnp.concatenate(
                    [ref[2 * pair, pl.ds(at, PART), :], ref[2 * pair + 1, pl.ds(at, PART), :]], axis=0
                )

            for p in range(4):
                lanes = slice(p * 128, (p + 1) * 128)
                pout[pair, j, pl.ds(p * ROWS, ROWS), :] = jnp.concatenate(
                    [acc[2 * pair, pl.ds(at, PART), lanes], acc[2 * pair + 1, pl.ds(at, PART), lanes]],
                    axis=0,
                ).astype(BF16)
            m, l = both(peak), both(total)
            m_high = m.astype(BF16).astype(F32)
            m_mid = (m - m_high).astype(BF16).astype(F32)
            m_low = m - m_high - m_mid
            l_high = l.astype(BF16).astype(F32)
            stats = jnp.zeros((16, 128), F32)
            for i in range(3):
                rows = slice(16 * i, 16 * (i + 1))
                for q, value in enumerate((m_high, m_mid, m_low, l_high, l - l_high)):
                    stats = jnp.where(lane == 8 * i + q, value[rows], stats)
            pout[pair, j, pl.ds(4 * ROWS, 16), :] = stats.astype(BF16)
            return carry

        lax.fori_loop(0, NSEQ, one, 0)

    def partial_copies(pair):
        return [
            pltpu.make_async_remote_copy(
                src_ref=pout.at[pair, j], dst_ref=pin.at[pair, (NZ - j // NX) % NZ * NX + (NX - j % NX) % NX],
                send_sem=p_ss.at[pair, j], recv_sem=p_rs.at[pair, j],
                device_id=seq_dev(j // NX, j % NX), device_id_type=MESH,
            )
            for j in range(1, NSEQ)
        ]

    def finish(pair):
        stats = jnp.concatenate(
            [pout[pair, 0, pl.ds(4 * ROWS, 16), :]]
            + [pin[pair, j, pl.ds(4 * ROWS, 16), :] for j in range(1, NSEQ)],
            axis=0,
        )
        source = lax.broadcasted_iota(jnp.int32, (128, 128), 0)
        picks = [
            ((source >= 8 * i) & (source < 8 * i + 3)).astype(F32).astype(BF16) for i in range(3)
        ] + [
            ((source >= 8 * i + 3) & (source < 8 * i + 5)).astype(F32).astype(BF16) for i in range(3)
        ]
        spread_stats = dot(stats, jnp.concatenate(picks, axis=1))

        def of(j, kind):
            return jnp.concatenate(
                [
                    spread_stats[16 * j : 16 * (j + 1), 128 * (3 * kind + i) : 128 * (3 * kind + i + 1)]
                    for i in range(3)
                ],
                axis=0,
            )

        rows = pl.ds(pair * ROWS, ROWS)
        peaks = [of(j, 0) for j in range(NSEQ)]
        m_fresh = fresh_m[rows, :]
        top = m_fresh
        for m in peaks:
            top = jnp.maximum(top, m)
        keep = jnp.exp2((m_fresh - top) * EXPC)
        sums = keep * fresh_l[rows, :]
        values = [keep * fresh_w[rows, p * 128 : (p + 1) * 128] for p in range(4)]
        for j in range(NSEQ):
            keep = jnp.exp2((peaks[j] - top) * EXPC)
            sums = sums + keep * of(j, 1)
            message = pout if j == 0 else pin
            for p in range(4):
                values[p] = values[p] + keep * message[pair, j, pl.ds(p * ROWS, ROWS), :].astype(F32)
        head = lax.broadcasted_iota(jnp.int32, (ROWS, 128), 0) & 7
        attended = [(v / sums).astype(BF16).astype(F32) for v in values]
        spread = [
            jnp.where(head == h, attended[p], 0.0).astype(BF16) for h in range(HEADS) for p in range(4)
        ]
        result = dot(jnp.concatenate(spread, axis=1), wv[...].reshape(HEADS * LAT, 128))
        out_ref[rows, :] = result.astype(BF16)

    arrived(others + forward_z0 + forward_x0)
    assemble(0)
    loads[2].wait()

    def resident(r, carry):
        limit = len_ref[r] - s * CTX
        tile = 512
        position = lax.broadcasted_iota(jnp.int32, (QROWS, tile), 1)
        running = jnp.full((QROWS, 128), NEG, F32)
        for k in range(CTX // tile):
            keys = pl.ds(k * tile, tile)
            sc = dot(qall[r, :, :ROW], cache[r, :, keys])
            sc = jnp.where(position < limit - k * tile, sc, NEG)
            scores[:, keys] = sc
            for i in range(tile // 128):
                running = jnp.maximum(running, sc[:, i * 128 : (i + 1) * 128])
        m = jnp.max(running, axis=1, keepdims=True)
        sums = jnp.zeros((QROWS, 128), F32)
        for k in range(CTX // tile):
            keys = pl.ds(k * tile, tile)
            w = jnp.exp2((scores[:, keys] - m) * EXPC)
            for i in range(tile // 128):
                sums = sums + w[:, i * 128 : (i + 1) * 128]
            weights[:, keys] = w.astype(BF16)
        acc[r] = dot_t(weights[...], cache[r, :LAT, :])
        peak[r] = jnp.broadcast_to(m, (QROWS, 128))
        total[r] = jnp.broadcast_to(jnp.sum(sums, axis=1, keepdims=True), (QROWS, 128))
        return carry

    lax.fori_loop(0, 2, resident, 0)
    pack(0)
    partials0 = start(partial_copies(0))

    arrived(others1 + forward_z1 + forward_x1)
    assemble(1)
    for r in (2, 3):
        acc[r] = jnp.zeros((QROWS, LAT), F32)
        peak[r] = jnp.full((QROWS, 128), NEG, F32)
        total[r] = jnp.zeros((QROWS, 128), F32)

    def blocks(i):
        keys = jnp.concatenate([kv[i, pl.ds(0, ROW), :], kv[i, pl.ds(ROW, ROW), :]], axis=1)
        tags = kv[i, pl.ds(2 * ROW, 16), :].astype(F32)
        tag = jnp.concatenate([tags[0:1, :], tags[8:9, :]], axis=1)
        for r in (2, 3):
            sc = dot(qall[r, :, :ROW], keys)
            sc = jnp.where(tag == float(r - 2), sc, NEG)
            old = peak[r]
            best = jnp.max(
                jnp.maximum(sc[:, :128], sc[:, 128:]), axis=1, keepdims=True
            )
            top = jnp.maximum(old, best)
            keep = jnp.exp2((old - top) * EXPC)
            w0 = jnp.exp2((sc[:, :128] - top) * EXPC)
            w1 = jnp.exp2((sc[:, 128:] - top) * EXPC)
            peak[r] = top
            total[r] = total[r] * keep + jnp.sum(w0 + w1, axis=1, keepdims=True)
            w = jnp.concatenate([w0, w1], axis=1).astype(BF16)
            term = dot_t(w, keys[:LAT])
            for p in range(4):
                lanes = slice(p * 128, (p + 1) * 128)
                acc[r, :, lanes] = acc[r, :, lanes] * keep + term[:, lanes]

    def landed(i, carry):
        pltpu.make_async_remote_copy(
            src_ref=ysend.at[i], dst_ref=kv.at[i], send_sem=y_ss.at[i], recv_sem=y_rs.at[i],
            device_id=(group_of(0, 1), s), device_id_type=MESH,
        ).wait_recv()
        blocks(i)
        return carry

    blocks(0)
    lax.fori_loop(1, 6, landed, 0)
    loads[3].wait()
    arrived(partials0)
    finish(0)
    lax.fori_loop(6, 8, landed, 0)
    pack(1)
    partials1 = start(partial_copies(1))
    arrived(partials1)
    finish(1)
    for copy in group_copies + sent + partials0 + partials1:
        copy.wait_send()


def body(q_nope, q_rope, w_absorb, w_value, cache, res_len, prefill_rows, block_dest, new_rows):
    rows = 4 * PART
    vmem, hbm, smem = (
        pl.BlockSpec(memory_space=pltpu.VMEM),
        pl.BlockSpec(memory_space=pl.ANY),
        pl.BlockSpec(memory_space=pltpu.SMEM),
    )
    out = pl.pallas_call(
        kernel,
        out_shape=jax.ShapeDtypeStruct((rows, 128), BF16),
        in_specs=[vmem, vmem, hbm, hbm, hbm, smem, hbm, smem, vmem],
        out_specs=vmem,
        scratch_shapes=[
            pltpu.VMEM(w_absorb.shape, BF16),
            pltpu.VMEM(w_value.shape, BF16),
            pltpu.VMEM((2, ROW, CTX), BF16),
            pltpu.VMEM((8, ROW, BLK), BF16),
            pltpu.VMEM((8, KMSG, 128), BF16),
            pltpu.VMEM((8, KMSG, 128), BF16),
            pltpu.VMEM((2, NZ, NX, QMSG, 128), BF16),
            pltpu.VMEM((4, QROWS, LAT + 128), BF16),
            pltpu.VMEM((QROWS, CTX), F32),
            pltpu.VMEM((QROWS, CTX), BF16),
            pltpu.VMEM((4, QROWS, LAT), F32),
            pltpu.VMEM((4, QROWS, 128), F32),
            pltpu.VMEM((4, QROWS, 128), F32),
            pltpu.VMEM((32, LAT + ROPE), F32),
            pltpu.VMEM((rows, LAT), F32),
            pltpu.VMEM((rows, 128), F32),
            pltpu.VMEM((rows, 128), F32),
            pltpu.VMEM((2, NSEQ, PMSG, 128), BF16),
            pltpu.VMEM((2, NSEQ, PMSG, 128), BF16),
            pltpu.SemaphoreType.DMA((4,)),
            pltpu.SemaphoreType.DMA((8,)),
            pltpu.SemaphoreType.DMA((8,)),
            pltpu.SemaphoreType.DMA((2, 12)),
            pltpu.SemaphoreType.DMA((2, 12)),
            pltpu.SemaphoreType.DMA((2, 6)),
            pltpu.SemaphoreType.DMA((2, 6)),
            pltpu.SemaphoreType.DMA((2, NSEQ)),
            pltpu.SemaphoreType.DMA((2, NSEQ)),
        ],
        compiler_params=pltpu.CompilerParams(
            collective_id=0, has_side_effects=True, vmem_limit_bytes=56 * 1024 * 1024
        ),
        name="latent_attention",
    )(
        q_nope.reshape(rows, 128),
        q_rope.reshape(rows, ROPE),
        w_absorb,
        w_value,
        cache.transpose(0, 2, 1),
        res_len,
        prefill_rows.transpose(0, 1, 3, 2),
        block_dest,
        new_rows.transpose(1, 0, 2),
    )
    return out.reshape(q_nope.shape)


def solution(mesh):
    in_specs = (
        P("group", None, "seq", None),
        P("group", None, "seq", None),
        P("seq", None, None),
        P("seq", None, None),
        P("group", "seq", None),
        P("group"),
        P("group", "seq", None, None),
        P("group", "seq"),
        P("group", None, None),
    )
    out_specs = P("group", None, "seq", None)
    return jax.shard_map(body, mesh=mesh, in_specs=in_specs, out_specs=out_specs, check_vma=False)
```

```python
import math

import jax
import jax.numpy as jnp
from jax import lax
from jax.experimental import pallas as pl
from jax.experimental.pallas import tpu as pltpu
from jax.sharding import PartitionSpec as P

MESH = pl.DeviceIdType.MESH
F32 = jnp.float32
BF16 = jnp.bfloat16

NY, NC, NZ, NX = 4, 2, 4, 4
HEADS = 8
STEPS = 3
PART = STEPS * HEADS
ROWS = 2 * PART
NSEQ = NZ * NX
QROWS = NSEQ * PART
LAT, ROPE = 512, 64
BLK = 128
CTX = 2048
QMSG = 5 * ROWS
QCUT = 128
PMSG = 4 * ROWS + 16
ROW = LAT + ROPE
KMSG = 2 * ROW + 16
NEG = -1e30
EXPC = (128 + 64) ** -0.5 * math.log2(math.e)

ALONG_Y = (1, 3, 2)


def dot_t(a, b):
    return lax.dot_general(a, b, (((1,), (1,)), ((), ())), preferred_element_type=F32)


def dot(a, b):
    return jnp.dot(a, b, preferred_element_type=F32)


def kernel(
    qn_hbm, qr_hbm, wa_hbm, wv_hbm, cache_hbm, len_hbm, pre_hbm, dest_hbm, new_hbm,
    out_ref,
    qn_ref, qr_ref, len_ref, dest_ref, new_ref, wa, wv, cache, pre, ysend, kv, qbuf, qall, scores, weights, acc, peak, total,
    fresh, fresh_w, fresh_m, fresh_l, pout, pin,
    local_sem, y_ss, y_rs, a_ss, a_rs, f_ss, f_rs, p_ss, p_rs,
):
    g, s = lax.axis_index("group"), lax.axis_index("seq")
    y, c = lax.div(g, NC), lax.rem(g, NC)
    z, x = lax.div(s, NX), lax.rem(s, NX)

    def group_dev(dy, core):
        return (lax.rem(y + dy, NY) * NC + core, s)

    def seq_dev(dz, dx):
        return (g, lax.rem(z + dz, NZ) * NX + lax.rem(x + dx, NX))

    loads = [
        pltpu.make_async_copy(src, dst, local_sem.at[i])
        for i, (src, dst) in enumerate(
            [
                (dest_hbm, dest_ref), (pre_hbm.at[0], pre), (qn_hbm, qn_ref), (qr_hbm, qr_ref), (wa_hbm, wa),
                (new_hbm, new_ref), (len_hbm, len_ref), (cache_hbm, cache), (wv_hbm, wv),
            ]
        )
    ]
    barrier = pltpu.get_barrier_semaphore()
    for load in loads[:5]:
        load.start()
    for device in (
        [group_dev(dy, core) for dy in ALONG_Y for core in range(NC)]
        + [group_dev(0, 1 - c)]
        + [seq_dev(j // NX, j % NX) for j in range(1, NSEQ)]
    ):
        pl.semaphore_signal(barrier, inc=1, device_id=device, device_id_type=MESH)
    for load in loads[5:]:
        load.start()

    loads[0].wait()
    owners = [dest_ref[0, k] for k in range(8)]
    targets = [lax.div(o, 2) for o in owners]
    members = [lax.rem(o, 2) for o in owners]
    tag_row = lax.broadcasted_iota(jnp.int32, (16, 128), 0)

    def pick(to, wanted):
        first = second = jnp.int32(0)
        tag_first = tag_second = jnp.int32(2)
        for k in reversed(range(8)):
            match = targets[k] == wanted
            second = jnp.where(match, first, second)
            tag_second = jnp.where(match, tag_first, tag_second)
            first = jnp.where(match, k, first)
            tag_first = jnp.where(match, members[k], tag_first)
        for slot, index in enumerate((first, second)):
            to[pl.ds(slot * ROW, ROW), :] = pre[index]
        tags = jnp.where(tag_row < 8, tag_first, tag_second)
        to[pl.ds(2 * ROW, 16), :] = tags.astype(F32).astype(BF16)

    def core_copy():
        return pltpu.make_async_remote_copy(
            src_ref=ysend.at[6], dst_ref=kv.at[1], send_sem=y_ss.at[6], recv_sem=y_rs.at[1],
            device_id=group_dev(0, 1 - c), device_id_type=MESH,
        )

    def y_copy(k, core):
        there = 2 + 2 * ALONG_Y.index((NY - ALONG_Y[k]) % NY) + c
        return pltpu.make_async_remote_copy(
            src_ref=ysend.at[3 * core + k], dst_ref=kv.at[there],
            send_sem=y_ss.at[3 * core + k], recv_sem=y_rs.at[there],
            device_id=group_dev(ALONG_Y[k], core), device_id_type=MESH,
        )

    def blocks_to(core):
        copies = [y_copy(k, core) for k in range(3)]
        for k, copy in enumerate(copies):
            pick(ysend.at[3 * core + k], lax.rem(y + ALONG_Y[k], NY) * NC + core)
            copy.start()
        return copies

    loads[1].wait()
    pl.semaphore_wait(barrier, 7 + NSEQ - 1)
    group_copies = blocks_to(0)

    for load in loads[2:5]:
        load.wait()
    row = lax.broadcasted_iota(jnp.int32, (2 * ROWS, 128), 0)
    own = qn_ref[...].astype(F32)
    spread = [jnp.where((row & 7) == h, own, 0.0).astype(BF16) for h in range(HEADS)]
    q_latent = dot(jnp.concatenate(spread, axis=1), wa[...].reshape(HEADS * 128, LAT))
    q_latent = q_latent.astype(BF16)
    q_rope = jnp.concatenate([qr_ref[...], jnp.zeros((2 * ROWS, 128 - ROPE), BF16)], axis=1)
    for pair in range(2):
        rows = slice(pair * ROWS, (pair + 1) * ROWS)
        for p in range(4):
            qbuf[pair, 0, 0, pl.ds(p * ROWS, ROWS), :] = q_latent[rows, p * 128 : (p + 1) * 128]
        qbuf[pair, 0, 0, pl.ds(4 * ROWS, ROWS), :] = q_rope[rows]

    low, high = pl.ds(0, QCUT), pl.ds(QCUT, QMSG - QCUT)

    def own_copy(pair, index, dz, dx, rows):
        return pltpu.make_async_remote_copy(
            src_ref=qbuf.at[pair, 0, 0, rows], dst_ref=qbuf.at[pair, (NZ - dz) % NZ, (NX - dx) % NX, rows],
            send_sem=a_ss.at[pair, index], recv_sem=a_rs.at[pair, index],
            device_id=seq_dev(dz, dx), device_id_type=MESH,
        )

    def x_first(pair):
        return [own_copy(pair, d - 1, 0, d, low) for d in (1, 2, 3)]

    def z_first(pair):
        return [own_copy(pair, 2 + d, d, 0, high) for d in (1, 2, 3)]

    def rest(pair):
        return [own_copy(pair, 5 + d, 0, d, high) for d in (1, 2, 3)] + [
            own_copy(pair, 8 + d, d, 0, low) for d in (1, 2, 3)
        ]

    def forward_z(pair):
        return [
            pltpu.make_async_remote_copy(
                src_ref=qbuf.at[pair, 0, pl.ds(1, 3), low], dst_ref=qbuf.at[pair, NZ - d, pl.ds(1, 3), low],
                send_sem=f_ss.at[pair, d - 1], recv_sem=f_rs.at[pair, d - 1],
                device_id=seq_dev(d, 0), device_id_type=MESH,
            )
            for d in (1, 2, 3)
        ]

    def forward_x(pair):
        return [
            pltpu.make_async_remote_copy(
                src_ref=qbuf.at[pair, pl.ds(1, 3), 0, high], dst_ref=qbuf.at[pair, pl.ds(1, 3), NX - d, high],
                send_sem=f_ss.at[pair, 2 + d], recv_sem=f_rs.at[pair, 2 + d],
                device_id=seq_dev(0, d), device_id_type=MESH,
            )
            for d in (1, 2, 3)
        ]

    def start(copies):
        for copy in copies:
            copy.start()
        return copies

    def arrived(copies):
        for copy in copies:
            copy.wait_recv()

    sent = []
    first_x, first_z = start(x_first(0)), start(z_first(0))
    others = start(rest(0))
    sent += first_x + first_z + others

    group_copies += blocks_to(1)
    pick(ysend.at[6], y * NC + 1 - c)
    group_copies += start([core_copy()])
    pick(kv.at[0], y * NC + c)

    loads[5].wait()
    fresh[...] = jnp.zeros_like(fresh)
    for u in range(STEPS):
        new = new_ref[u].astype(F32)
        for r in range(4):
            fresh[pl.ds(8 * r + u, 1), :] = new[r : r + 1]
    fresh_rows = fresh[...].astype(BF16)
    s_fresh = dot_t(q_latent, fresh_rows[:, :LAT]) + dot_t(
        qr_ref[...], fresh_rows[:, LAT : LAT + ROPE]
    )
    part = lax.broadcasted_iota(jnp.int32, (2 * ROWS, 32), 0) >> 3
    key = lax.broadcasted_iota(jnp.int32, (2 * ROWS, 32), 1)
    request = (
        (part >= 3).astype(jnp.int32) + (part >= 6).astype(jnp.int32) + (part >= 9).astype(jnp.int32)
    )
    step = part - 3 * request
    allowed = ((key >> 3) == request) & ((key & 7) <= step)
    s_fresh = jnp.where(allowed, s_fresh, NEG)
    m_fresh = jnp.max(s_fresh, axis=1, keepdims=True)
    p_fresh = jnp.where(allowed, jnp.exp2((s_fresh - m_fresh) * EXPC), 0.0)
    fresh_m[...] = jnp.broadcast_to(m_fresh, fresh_m.shape)
    fresh_l[...] = jnp.broadcast_to(jnp.sum(p_fresh, axis=1, keepdims=True), fresh_l.shape)
    fresh_w[...] = dot(p_fresh.astype(BF16), fresh_rows[:, :LAT])

    arrived(first_x)
    sent += (forward_z0 := start(forward_z(0)))
    arrived(first_z)
    sent += (forward_x0 := start(forward_x(0)))
    first_x1, first_z1 = start(x_first(1)), start(z_first(1))
    others1 = start(rest(1))
    sent += first_x1 + first_z1 + others1
    arrived(first_x1)
    sent += (forward_z1 := start(forward_z(1)))
    arrived(first_z1)
    sent += (forward_x1 := start(forward_x(1)))

    def assemble(pair):
        def two(i, carry):
            at = pl.multiple_of(i * 2 * PART, 16)
            dz, dx = lax.div(i, 2), lax.rem(i, 2) * 2
            for p in range(5):
                one = qbuf[pair, dz, dx, pl.ds(p * ROWS, ROWS), :].astype(F32)
                two = qbuf[pair, dz, dx + 1, pl.ds(p * ROWS, ROWS), :].astype(F32)
                lanes = slice(p * 128, (p + 1) * 128)
                for r in range(2):
                    rows = slice(r * PART, (r + 1) * PART)
                    qall[2 * pair + r, pl.ds(at, 2 * PART), lanes] = jnp.concatenate(
                        [one[rows], two[rows]], axis=0
                    ).astype(BF16)
            return carry

        lax.fori_loop(0, NSEQ // 2, two, 0)

    def pack(pair):
        lane = lax.broadcasted_iota(jnp.int32, (16, 128), 1)

        def one(j, carry):
            at = pl.multiple_of(j * PART, 8)

            def both(ref):
                return jnp.concatenate(
                    [ref[2 * pair, pl.ds(at, PART), :], ref[2 * pair + 1, pl.ds(at, PART), :]], axis=0
                )

            for p in range(4):
                lanes = slice(p * 128, (p + 1) * 128)
                pout[pair, j, pl.ds(p * ROWS, ROWS), :] = jnp.concatenate(
                    [acc[2 * pair, pl.ds(at, PART), lanes], acc[2 * pair + 1, pl.ds(at, PART), lanes]],
                    axis=0,
                ).astype(BF16)
            m, l = both(peak), both(total)
            m_high = m.astype(BF16).astype(F32)
            m_mid = (m - m_high).astype(BF16).astype(F32)
            m_low = m - m_high - m_mid
            l_high = l.astype(BF16).astype(F32)
            stats = jnp.zeros((16, 128), F32)
            for i in range(3):
                rows = slice(16 * i, 16 * (i + 1))
                for q, value in enumerate((m_high, m_mid, m_low, l_high, l - l_high)):
                    stats = jnp.where(lane == 8 * i + q, value[rows], stats)
            pout[pair, j, pl.ds(4 * ROWS, 16), :] = stats.astype(BF16)
            return carry

        lax.fori_loop(0, NSEQ, one, 0)

    def partial_copies(pair):
        return [
            pltpu.make_async_remote_copy(
                src_ref=pout.at[pair, j], dst_ref=pin.at[pair, (NZ - j // NX) % NZ * NX + (NX - j % NX) % NX],
                send_sem=p_ss.at[pair, j], recv_sem=p_rs.at[pair, j],
                device_id=seq_dev(j // NX, j % NX), device_id_type=MESH,
            )
            for j in range(1, NSEQ)
        ]

    def finish(pair):
        stats = jnp.concatenate(
            [pout[pair, 0, pl.ds(4 * ROWS, 16), :]]
            + [pin[pair, j, pl.ds(4 * ROWS, 16), :] for j in range(1, NSEQ)],
            axis=0,
        )
        source = lax.broadcasted_iota(jnp.int32, (128, 128), 0)
        picks = [
            ((source >= 8 * i) & (source < 8 * i + 3)).astype(F32).astype(BF16) for i in range(3)
        ] + [
            ((source >= 8 * i + 3) & (source < 8 * i + 5)).astype(F32).astype(BF16) for i in range(3)
        ]
        spread_stats = dot(stats, jnp.concatenate(picks, axis=1))

        def of(j, kind):
            return jnp.concatenate(
                [
                    spread_stats[16 * j : 16 * (j + 1), 128 * (3 * kind + i) : 128 * (3 * kind + i + 1)]
                    for i in range(3)
                ],
                axis=0,
            )

        rows = pl.ds(pair * ROWS, ROWS)
        peaks = [of(j, 0) for j in range(NSEQ)]
        m_fresh = fresh_m[rows, :]
        top = m_fresh
        for m in peaks:
            top = jnp.maximum(top, m)
        keep = jnp.exp2((m_fresh - top) * EXPC)
        sums = keep * fresh_l[rows, :]
        values = [keep * fresh_w[rows, p * 128 : (p + 1) * 128] for p in range(4)]
        for j in range(NSEQ):
            keep = jnp.exp2((peaks[j] - top) * EXPC)
            sums = sums + keep * of(j, 1)
            message = pout if j == 0 else pin
            for p in range(4):
                values[p] = values[p] + keep * message[pair, j, pl.ds(p * ROWS, ROWS), :].astype(F32)
        head = lax.broadcasted_iota(jnp.int32, (ROWS, 128), 0) & 7
        attended = [(v / sums).astype(BF16).astype(F32) for v in values]
        spread = [
            jnp.where(head == h, attended[p], 0.0).astype(BF16) for h in range(HEADS) for p in range(4)
        ]
        result = dot(jnp.concatenate(spread, axis=1), wv[...].reshape(HEADS * LAT, 128))
        out_ref[rows, :] = result.astype(BF16)

    arrived(others + forward_z0 + forward_x0)
    assemble(0)
    loads[6].wait()
    loads[7].wait()

    def resident(r, carry):
        limit = len_ref[r] - s * CTX
        tile = 512
        position = lax.broadcasted_iota(jnp.int32, (QROWS, tile), 1)
        running = jnp.full((QROWS, 128), NEG, F32)
        for k in range(CTX // tile):
            keys = pl.ds(k * tile, tile)
            sc = dot(qall[r, :, :ROW], cache[r, :, keys])
            sc = jnp.where(position < limit - k * tile, sc, NEG)
            scores[:, keys] = sc
            for i in range(tile // 128):
                running = jnp.maximum(running, sc[:, i * 128 : (i + 1) * 128])
        m = jnp.max(running, axis=1, keepdims=True)
        sums = jnp.zeros((QROWS, 128), F32)
        for k in range(CTX // tile):
            keys = pl.ds(k * tile, tile)
            w = jnp.exp2((scores[:, keys] - m) * EXPC)
            for i in range(tile // 128):
                sums = sums + w[:, i * 128 : (i + 1) * 128]
            weights[:, keys] = w.astype(BF16)
        acc[r] = dot_t(weights[...], cache[r, :LAT, :])
        peak[r] = jnp.broadcast_to(m, (QROWS, 128))
        total[r] = jnp.broadcast_to(jnp.sum(sums, axis=1, keepdims=True), (QROWS, 128))
        return carry

    lax.fori_loop(0, 2, resident, 0)
    pack(0)
    partials0 = start(partial_copies(0))

    arrived(others1 + forward_z1 + forward_x1)
    assemble(1)
    for r in (2, 3):
        acc[r] = jnp.zeros((QROWS, LAT), F32)
        peak[r] = jnp.full((QROWS, 128), NEG, F32)
        total[r] = jnp.zeros((QROWS, 128), F32)

    def blocks(i):
        keys = jnp.concatenate(
            [kv[i + n // 2, pl.ds(n % 2 * ROW, ROW), :] for n in range(4)], axis=1
        )
        tags = [kv[i + n, pl.ds(2 * ROW, 16), :].astype(F32) for n in range(2)]
        tag = jnp.concatenate([tags[n // 2][n % 2 * 8 : n % 2 * 8 + 1, :] for n in range(4)], axis=1)
        for r in (2, 3):
            sc = dot(qall[r, :, :ROW], keys)
            sc = jnp.where(tag == float(r - 2), sc, NEG)
            old = peak[r]
            best = jnp.maximum(
                jnp.maximum(sc[:, :128], sc[:, 128:256]), jnp.maximum(sc[:, 256:384], sc[:, 384:])
            )
            top = jnp.maximum(old, jnp.max(best, axis=1, keepdims=True))
            keep = jnp.exp2((old - top) * EXPC)
            w = [jnp.exp2((sc[:, n * 128 : (n + 1) * 128] - top) * EXPC) for n in range(4)]
            peak[r] = top
            total[r] = total[r] * keep + jnp.sum((w[0] + w[1]) + (w[2] + w[3]), axis=1, keepdims=True)
            w = jnp.concatenate(w, axis=1).astype(BF16)
            term = dot_t(w, keys[:LAT])
            for p in range(4):
                lanes = slice(p * 128, (p + 1) * 128)
                acc[r, :, lanes] = acc[r, :, lanes] * keep + term[:, lanes]

    def landed(i):
        pltpu.make_async_remote_copy(
            src_ref=ysend.at[6], dst_ref=kv.at[i], send_sem=y_ss.at[6], recv_sem=y_rs.at[i],
            device_id=group_dev(0, 1 - c), device_id_type=MESH,
        ).wait_recv()

    landed(1)
    blocks(0)

    def four(k, carry):
        landed(2 * k)
        landed(2 * k + 1)
        blocks(2 * k)
        return carry

    lax.fori_loop(1, 4, four, 0)
    pack(1)
    partials1 = start(partial_copies(1))
    loads[8].wait()
    arrived(partials0)
    finish(0)
    arrived(partials1)
    finish(1)
    for copy in group_copies + sent + partials0 + partials1:
        copy.wait_send()


def body(q_nope, q_rope, w_absorb, w_value, cache, res_len, prefill_rows, block_dest, new_rows):
    rows = 4 * PART
    out = pl.pallas_call(
        kernel,
        out_shape=jax.ShapeDtypeStruct((rows, 128), BF16),
        in_specs=[pl.BlockSpec(memory_space=pl.ANY)] * 9,
        out_specs=pl.BlockSpec(memory_space=pltpu.VMEM),
        scratch_shapes=[
            pltpu.VMEM((rows, 128), BF16),
            pltpu.VMEM((rows, ROPE), BF16),
            pltpu.SMEM(res_len.shape, jnp.int32),
            pltpu.SMEM(block_dest.shape, jnp.int32),
            pltpu.VMEM((STEPS, 4, ROW), BF16),
            pltpu.VMEM(w_absorb.shape, BF16),
            pltpu.VMEM(w_value.shape, BF16),
            pltpu.VMEM((2, ROW, CTX), BF16),
            pltpu.VMEM((8, ROW, BLK), BF16),
            pltpu.VMEM((7, KMSG, 128), BF16),
            pltpu.VMEM((8, KMSG, 128), BF16),
            pltpu.VMEM((2, NZ, NX, QMSG, 128), BF16),
            pltpu.VMEM((4, QROWS, LAT + 128), BF16),
            pltpu.VMEM((QROWS, CTX), F32),
            pltpu.VMEM((QROWS, CTX), BF16),
            pltpu.VMEM((4, QROWS, LAT), F32),
            pltpu.VMEM((4, QROWS, 128), F32),
            pltpu.VMEM((4, QROWS, 128), F32),
            pltpu.VMEM((32, LAT + ROPE), F32),
            pltpu.VMEM((rows, LAT), F32),
            pltpu.VMEM((rows, 128), F32),
            pltpu.VMEM((rows, 128), F32),
            pltpu.VMEM((2, NSEQ, PMSG, 128), BF16),
            pltpu.VMEM((2, NSEQ, PMSG, 128), BF16),
            pltpu.SemaphoreType.DMA((9,)),
            pltpu.SemaphoreType.DMA((7,)),
            pltpu.SemaphoreType.DMA((8,)),
            pltpu.SemaphoreType.DMA((2, 12)),
            pltpu.SemaphoreType.DMA((2, 12)),
            pltpu.SemaphoreType.DMA((2, 6)),
            pltpu.SemaphoreType.DMA((2, 6)),
            pltpu.SemaphoreType.DMA((2, NSEQ)),
            pltpu.SemaphoreType.DMA((2, NSEQ)),
        ],
        compiler_params=pltpu.CompilerParams(
            collective_id=0, has_side_effects=True, vmem_limit_bytes=56 * 1024 * 1024
        ),
        name="latent_attention",
    )(
        q_nope.reshape(rows, 128),
        q_rope.reshape(rows, ROPE),
        w_absorb,
        w_value,
        cache.transpose(0, 2, 1),
        res_len,
        prefill_rows.transpose(0, 1, 3, 2),
        block_dest,
        new_rows.transpose(1, 0, 2),
    )
    return out.reshape(q_nope.shape)


def solution(mesh):
    in_specs = (
        P("group", None, "seq", None),
        P("group", None, "seq", None),
        P("seq", None, None),
        P("seq", None, None),
        P("group", "seq", None),
        P("group"),
        P("group", "seq", None, None),
        P("group", "seq"),
        P("group", None, None),
    )
    out_specs = P("group", None, "seq", None)
    return jax.shard_map(body, mesh=mesh, in_specs=in_specs, out_specs=out_specs, check_vma=False)
```

```python
import functools
import math

import jax
import jax.numpy as jnp
from jax import lax
from jax.experimental import pallas as pl
from jax.experimental.pallas import tpu as pltpu
from jax.sharding import PartitionSpec as P

MESH = pl.DeviceIdType.MESH
F32 = jnp.float32
BF16 = jnp.bfloat16

NY, NC, NZ, NX = 4, 2, 4, 4
HEADS = 8
STEPS = 3
PART = STEPS * HEADS
ROWS = 2 * PART
NSEQ = NZ * NX
QROWS = NSEQ * PART
LAT, ROPE = 512, 64
BLK = 128
CTX = 2048
QMSG = 4 * ROWS + 32
QCUT = QMSG // 2
PMSG = 4 * ROWS + 16
ROW = LAT + ROPE
KMSG = 16 + 2 * ROW
NEG = -1e30
EXPC = (128 + 64) ** -0.5 * math.log2(math.e)

ALONG_Y = (1, 3, 2)
FAR_FIRST = [
    (1, 2), (2, 1), (3, 2), (2, 3), (2, 2), (1, 1), (3, 3), (1, 3), (3, 1), (0, 2), (2, 0), (0, 1), (1, 0), (0, 3), (3, 0),
]


def dot_t(a, b):
    return lax.dot_general(a, b, (((1,), (1,)), ((), ())), preferred_element_type=F32)


def dot(a, b):
    return jnp.dot(a, b, preferred_element_type=F32)


def kernel(
    qn_hbm, qr_hbm, wa_hbm, wv_hbm, cache_hbm, len_hbm, pre_hbm, dest_hbm, new_hbm,
    out_ref,
    qn_ref, qr_ref, len_ref, dest_ref, new_ref, wa, wv, cache, pre, ysend, kv, qbuf, qall, scores, weights, acc, peak, total,
    fresh, fresh_w, fresh_m, fresh_l, pout, pin,
    local_sem, y_ss, y_rs, a_ss, a_rs, f_ss, f_rs, p_ss, p_rs,
):
    g, s = lax.axis_index("group"), lax.axis_index("seq")
    y, c = lax.div(g, NC), lax.rem(g, NC)
    z, x = lax.div(s, NX), lax.rem(s, NX)

    def group_dev(dy, core):
        return (lax.rem(y + dy, NY) * NC + core, s)

    def seq_dev(dz, dx):
        return (g, lax.rem(z + dz, NZ) * NX + lax.rem(x + dx, NX))

    loads = [
        pltpu.make_async_copy(src, dst, local_sem.at[i])
        for i, (src, dst) in enumerate(
            [
                (dest_hbm, dest_ref), (pre_hbm.at[0], pre), (qn_hbm, qn_ref), (qr_hbm, qr_ref), (wa_hbm, wa),
                (new_hbm, new_ref), (len_hbm, len_ref), (cache_hbm, cache), (wv_hbm, wv),
            ]
        )
    ]
    barrier = pltpu.get_barrier_semaphore()
    for load in loads[:5]:
        load.start()
    for device in (
        [group_dev(dy, core) for dy in ALONG_Y for core in range(NC)]
        + [group_dev(0, 1 - c)]
        + [seq_dev(j // NX, j % NX) for j in range(1, NSEQ)]
    ):
        pl.semaphore_signal(barrier, inc=1, device_id=device, device_id_type=MESH)

    for load in loads[5:]:
        load.start()

    def start(copies):
        for copy in copies:
            copy.start()
        return copies

    loads[0].wait()
    owners = [dest_ref[0, k] for k in range(8)]
    targets = [lax.div(o, 2) for o in owners]
    members = [lax.rem(o, 2) for o in owners]
    tag_row = lax.broadcasted_iota(jnp.int32, (16, 128), 0)

    def pick(to, wanted):
        first = second = jnp.int32(0)
        tag_first = tag_second = jnp.int32(2)
        for k in reversed(range(8)):
            match = targets[k] == wanted
            second = jnp.where(match, first, second)
            tag_second = jnp.where(match, tag_first, tag_second)
            first = jnp.where(match, k, first)
            tag_first = jnp.where(match, members[k], tag_first)
        for slot, index in enumerate((first, second)):
            to[pl.ds(16 + slot * ROW, ROW), :] = pre[index]
        tags = jnp.where(tag_row < 8, tag_first, tag_second)
        to[pl.ds(0, 16), :] = tags.astype(F32).astype(BF16)

    def core_copy():
        return pltpu.make_async_remote_copy(
            src_ref=ysend.at[6], dst_ref=kv.at[1], send_sem=y_ss.at[6], recv_sem=y_rs.at[1],
            device_id=group_dev(0, 1 - c), device_id_type=MESH,
        )

    parts = [pl.ds(0, KMSG), pl.ds(0, 16 + ROW), pl.ds(16 + ROW, ROW)]

    def y_copy(k, core, part):
        there = 2 + 2 * ALONG_Y.index((NY - ALONG_Y[k]) % NY) + c
        late = 2 if part == 2 else 0
        return pltpu.make_async_remote_copy(
            src_ref=ysend.at[3 * core + k, parts[part]], dst_ref=kv.at[there, parts[part]],
            send_sem=y_ss.at[3 * core + k + (5 - 2 * core if late else 0)], recv_sem=y_rs.at[there + late],
            device_id=group_dev(ALONG_Y[k], core), device_id_type=MESH,
        )

    def blocks_to(core):
        copies = []
        for k in range(3):
            pick(ysend.at[3 * core + k], lax.rem(y + ALONG_Y[k], NY) * NC + core)
            copies += start([y_copy(k, core, part) for part in ((0,) if k < 2 else (1, 2))])
        return copies

    loads[1].wait()
    pl.semaphore_wait(barrier, 2 * NY - 1 + NSEQ - 1)

    group_copies = blocks_to(0)

    for load in loads[2:5]:
        load.wait()
    row = lax.broadcasted_iota(jnp.int32, (2 * ROWS, 128), 0)
    own = qn_ref[...].astype(F32)
    spread = [jnp.where((row & 7) == h, own, 0.0).astype(BF16) for h in range(HEADS)]
    q_latent = dot(jnp.concatenate(spread, axis=1), wa[...].reshape(HEADS * 128, LAT))
    q_latent = q_latent.astype(BF16)
    for pair in range(2):
        rows = slice(pair * ROWS, (pair + 1) * ROWS)
        for p in range(4):
            qbuf[pair, 0, 0, pl.ds(p * ROWS, ROWS), :] = q_latent[rows, p * 128 : (p + 1) * 128]
        ropes = [qr_ref[pl.ds(pair * ROWS + 16 * i, 16), :] for i in range(3)]
        ropes.append(jnp.zeros((16, ROPE), BF16))
        for i in range(2):
            qbuf[pair, 0, 0, pl.ds(4 * ROWS + 16 * i, 16), :] = jnp.concatenate(
                ropes[2 * i : 2 * i + 2], axis=1
            )

    low, high = pl.ds(0, QCUT), pl.ds(QCUT, QMSG - QCUT)

    def own_copy(pair, index, dz, dx, rows):
        return pltpu.make_async_remote_copy(
            src_ref=qbuf.at[pair, 0, 0, rows], dst_ref=qbuf.at[pair, (NZ - dz) % NZ, (NX - dx) % NX, rows],
            send_sem=a_ss.at[pair, index], recv_sem=a_rs.at[pair, index],
            device_id=seq_dev(dz, dx), device_id_type=MESH,
        )

    def x_first(pair):
        return [own_copy(pair, d - 1, 0, d, low) for d in (1, 2, 3)]

    def z_first(pair):
        return [own_copy(pair, 2 + d, d, 0, high) for d in (1, 2, 3)]

    def rest(pair):
        return [own_copy(pair, 5 + d, 0, d, high) for d in (1, 2, 3)] + [
            own_copy(pair, 8 + d, d, 0, low) for d in (1, 2, 3)
        ]

    def forward_z(pair):
        return [
            pltpu.make_async_remote_copy(
                src_ref=qbuf.at[pair, 0, pl.ds(1, 3), low], dst_ref=qbuf.at[pair, NZ - d, pl.ds(1, 3), low],
                send_sem=f_ss.at[pair, d - 1], recv_sem=f_rs.at[pair, d - 1],
                device_id=seq_dev(d, 0), device_id_type=MESH,
            )
            for d in (1, 2, 3)
        ]

    def forward_x(pair):
        return [
            pltpu.make_async_remote_copy(
                src_ref=qbuf.at[pair, pl.ds(1, 3), 0, high], dst_ref=qbuf.at[pair, pl.ds(1, 3), NX - d, high],
                send_sem=f_ss.at[pair, 2 + d], recv_sem=f_rs.at[pair, 2 + d],
                device_id=seq_dev(0, d), device_id_type=MESH,
            )
            for d in (1, 2, 3)
        ]

    def arrived(copies):
        for copy in copies:
            copy.wait_recv()

    sent = []
    first_x, first_z = start(x_first(0)), start(z_first(0))
    others = start(rest(0))
    sent += first_x + first_z + others

    group_copies += blocks_to(1)
    pick(ysend.at[6], y * NC + 1 - c)
    group_copies += start([core_copy()])
    pick(kv.at[0], y * NC + c)

    loads[5].wait()
    fresh[...] = jnp.zeros_like(fresh)
    for u in range(STEPS):
        new = new_ref[u].astype(F32)
        for r in range(4):
            fresh[pl.ds(8 * r + u, 1), :] = new[r : r + 1]
    fresh_rows = fresh[...].astype(BF16)
    s_fresh = dot_t(q_latent, fresh_rows[:, :LAT]) + dot_t(
        qr_ref[...], fresh_rows[:, LAT : LAT + ROPE]
    )
    part = lax.broadcasted_iota(jnp.int32, (2 * ROWS, 32), 0) >> 3
    key = lax.broadcasted_iota(jnp.int32, (2 * ROWS, 32), 1)
    request = (
        (part >= 3).astype(jnp.int32) + (part >= 6).astype(jnp.int32) + (part >= 9).astype(jnp.int32)
    )
    step = part - 3 * request
    allowed = ((key >> 3) == request) & ((key & 7) <= step)
    s_fresh = jnp.where(allowed, s_fresh, NEG)
    m_fresh = jnp.max(s_fresh, axis=1, keepdims=True)
    p_fresh = jnp.where(allowed, jnp.exp2((s_fresh - m_fresh) * EXPC), 0.0)
    fresh_m[...] = jnp.broadcast_to(m_fresh, fresh_m.shape)
    fresh_l[...] = jnp.broadcast_to(jnp.sum(p_fresh, axis=1, keepdims=True), fresh_l.shape)
    fresh_w[...] = dot(p_fresh.astype(BF16), fresh_rows[:, :LAT])

    arrived(first_x)
    sent += (forward_z0 := start(forward_z(0)))
    arrived(first_z)
    sent += (forward_x0 := start(forward_x(0)))
    first_x1, first_z1 = start(x_first(1)), start(z_first(1))
    others1 = start(rest(1))
    sent += first_x1 + first_z1 + others1
    arrived(first_x1)
    sent += (forward_z1 := start(forward_z(1)))
    arrived(first_z1)
    sent += (forward_x1 := start(forward_x(1)))

    def assemble(pair):
        def two(i, carry):
            at = pl.multiple_of(i * 2 * PART, 16)
            dz, dx = lax.div(i, 2), lax.rem(i, 2) * 2
            def part(d, p):
                if p < 4:
                    return qbuf[pair, dz, dx + d, pl.ds(p * ROWS, ROWS), :].astype(F32)
                first, second = (
                    qbuf[pair, dz, dx + d, pl.ds(4 * ROWS + 16 * i, 16), :].astype(F32) for i in range(2)
                )
                return jnp.concatenate([first, pltpu.roll(first, ROPE, 1), second], axis=0)

            for p in range(5):
                one, two = part(0, p), part(1, p)
                lanes = slice(p * 128, (p + 1) * 128)
                for r in range(2):
                    rows = slice(r * PART, (r + 1) * PART)
                    qall[2 * pair + r, pl.ds(at, 2 * PART), lanes] = jnp.concatenate(
                        [one[rows], two[rows]], axis=0
                    ).astype(BF16)
            return carry

        lax.fori_loop(0, NSEQ // 2, two, 0)

    def pack(pair):
        lane = lax.broadcasted_iota(jnp.int32, (16, 128), 1)

        def one(j, carry):
            at = pl.multiple_of(j * PART, 8)

            def both(ref):
                return jnp.concatenate(
                    [ref[2 * pair, pl.ds(at, PART), :], ref[2 * pair + 1, pl.ds(at, PART), :]], axis=0
                )

            for p in range(4):
                lanes = slice(p * 128, (p + 1) * 128)
                pout[pair, j, pl.ds(p * ROWS, ROWS), :] = jnp.concatenate(
                    [acc[2 * pair, pl.ds(at, PART), lanes], acc[2 * pair + 1, pl.ds(at, PART), lanes]],
                    axis=0,
                ).astype(BF16)
            m, l = both(peak), both(total)
            m_high = m.astype(BF16).astype(F32)
            m_mid = (m - m_high).astype(BF16).astype(F32)
            m_low = m - m_high - m_mid
            l_high = l.astype(BF16).astype(F32)
            stats = jnp.zeros((16, 128), F32)
            for i in range(3):
                rows = slice(16 * i, 16 * (i + 1))
                for q, value in enumerate((m_high, m_mid, m_low, l_high, l - l_high)):
                    stats = jnp.where(lane == 8 * i + q, value[rows], stats)
            pout[pair, j, pl.ds(4 * ROWS, 16), :] = stats.astype(BF16)
            return carry

        lax.fori_loop(0, NSEQ, one, 0)

    def partial_copy(pair, j):
        dz, dx = lax.div(j, NX), lax.rem(j, NX)
        there = lax.rem(NZ - dz, NZ) * NX + lax.rem(NX - dx, NX)
        return pltpu.make_async_remote_copy(
            src_ref=pout.at[pair, j], dst_ref=pin.at[pair, there],
            send_sem=p_ss.at[pair, j], recv_sem=p_rs.at[pair, there],
            device_id=seq_dev(dz, dx), device_id_type=MESH,
        )

    def partial_copies(pair):
        return [partial_copy(pair, dz * NX + dx) for dz, dx in FAR_FIRST]

    def finish(pair):
        stats = jnp.concatenate(
            [pout[pair, 0, pl.ds(4 * ROWS, 16), :]]
            + [pin[pair, j, pl.ds(4 * ROWS, 16), :] for j in range(1, NSEQ)],
            axis=0,
        )
        source = lax.broadcasted_iota(jnp.int32, (128, 128), 0)
        picks = [
            ((source >= 8 * i) & (source < 8 * i + 3)).astype(F32).astype(BF16) for i in range(3)
        ] + [
            ((source >= 8 * i + 3) & (source < 8 * i + 5)).astype(F32).astype(BF16) for i in range(3)
        ]
        spread_stats = dot(stats, jnp.concatenate(picks, axis=1))

        def of(j, kind):
            return jnp.concatenate(
                [
                    spread_stats[16 * j : 16 * (j + 1), 128 * (3 * kind + i) : 128 * (3 * kind + i + 1)]
                    for i in range(3)
                ],
                axis=0,
            )

        rows = pl.ds(pair * ROWS, ROWS)
        peaks = [of(j, 0) for j in range(NSEQ)]
        m_fresh = fresh_m[rows, :]
        top = m_fresh
        for m in peaks:
            top = jnp.maximum(top, m)
        keep = jnp.exp2((m_fresh - top) * EXPC)
        sums = keep * fresh_l[rows, :]
        values = [keep * fresh_w[rows, p * 128 : (p + 1) * 128] for p in range(4)]
        for j in range(NSEQ):
            keep = jnp.exp2((peaks[j] - top) * EXPC)
            sums = sums + keep * of(j, 1)
            message = pout if j == 0 else pin
            for p in range(4):
                values[p] = values[p] + keep * message[pair, j, pl.ds(p * ROWS, ROWS), :].astype(F32)
        head = lax.broadcasted_iota(jnp.int32, (ROWS, 128), 0) & 7
        attended = [(v / sums).astype(BF16).astype(F32) for v in values]
        spread = [
            jnp.where(head == h, attended[p], 0.0).astype(BF16) for h in range(HEADS) for p in range(4)
        ]
        result = dot(jnp.concatenate(spread, axis=1), wv[...].reshape(HEADS * LAT, 128))
        out_ref[rows, :] = result.astype(BF16)

    arrived(others + forward_z0 + forward_x0)
    assemble(0)
    loads[6].wait()
    loads[7].wait()

    tile = 512
    tiles = range(CTX // tile)
    position = lax.broadcasted_iota(jnp.int32, (QROWS, tile), 1)

    def score(r, k, running):
        keys = pl.ds(k * tile, tile)
        sc = dot(qall[r, :, :ROW], cache[r, :, keys])
        sc = jnp.where(position < len_ref[r] - s * CTX - k * tile, sc, NEG)
        scores[r, :, keys] = sc
        for i in range(tile // 128):
            running = jnp.maximum(running, sc[:, i * 128 : (i + 1) * 128])
        return running

    def weigh(r, k, m, sums):
        keys = pl.ds(k * tile, tile)
        w = jnp.exp2((scores[r, :, keys] - m) * EXPC)
        for i in range(tile // 128):
            sums = sums + w[:, i * 128 : (i + 1) * 128]
        weights[r, :, keys] = w.astype(BF16)
        return sums

    def done(r, m, sums):
        peak[r] = jnp.broadcast_to(m, (QROWS, 128))
        total[r] = jnp.broadcast_to(jnp.sum(sums, axis=1, keepdims=True), (QROWS, 128))

    lowest, nothing = jnp.full((QROWS, 128), NEG, F32), jnp.zeros((QROWS, 128), F32)
    m0 = m1 = lowest
    for k in tiles:
        m0 = score(0, k, m0)
    m0 = jnp.max(m0, axis=1, keepdims=True)
    sums0 = sums1 = nothing
    for k in tiles:
        m1 = score(1, k, m1)
        sums0 = weigh(0, k, m0, sums0)
    m1 = jnp.max(m1, axis=1, keepdims=True)
    done(0, m0, sums0)
    acc[0] = dot_t(weights[0], cache[0, :LAT, :])
    for k in tiles:
        sums1 = weigh(1, k, m1, sums1)
    done(1, m1, sums1)
    acc[1] = dot_t(weights[1], cache[1, :LAT, :])
    pack(0)
    partials0 = start(partial_copies(0))

    arrived(others1 + forward_z1 + forward_x1)
    assemble(1)
    for r in (2, 3):
        acc[r] = jnp.zeros((QROWS, LAT), F32)
        peak[r] = jnp.full((QROWS, 128), NEG, F32)
        total[r] = jnp.zeros((QROWS, 128), F32)

    def blocks(taken):
        keys = jnp.concatenate([kv[i, pl.ds(16 + slot * ROW, ROW), :] for i, slot in taken], axis=1)
        tag = jnp.concatenate(
            [kv[i, pl.ds(0, 16), :].astype(F32)[8 * slot : 8 * slot + 1] for i, slot in taken], axis=1
        )
        count = len(taken)
        new = (2, 3)
        scs = [jnp.where(tag == float(r - 2), dot(qall[r, :, :ROW], keys), NEG) for r in new]
        pieces = [[sc[:, n * 128 : (n + 1) * 128] for n in range(count)] for sc in scs]
        olds = [peak[r] for r in new]
        tops = [
            jnp.maximum(old, jnp.max(functools.reduce(jnp.maximum, some), axis=1, keepdims=True))
            for old, some in zip(olds, pieces)
        ]
        ws = [[jnp.exp2((piece - top) * EXPC) for piece in some] for some, top in zip(pieces, tops)]
        terms = [dot_t(jnp.concatenate(w, axis=1).astype(BF16), keys[:LAT]) for w in ws]
        for r, old, top, w, term in zip(new, olds, tops, ws, terms):
            keep = jnp.exp2((old - top) * EXPC)
            peak[r] = top
            total[r] = total[r] * keep + jnp.sum(sum(w[1:], w[0]), axis=1, keepdims=True)
            for p in range(4):
                lanes = slice(p * 128, (p + 1) * 128)
                acc[r, :, lanes] = acc[r, :, lanes] * keep + term[:, lanes]

    def landed(i, part, sem):
        pltpu.make_async_remote_copy(
            src_ref=ysend.at[6, parts[part]], dst_ref=kv.at[i, parts[part]],
            send_sem=y_ss.at[6], recv_sem=y_rs.at[sem],
            device_id=group_dev(0, 1 - c), device_id_type=MESH,
        ).wait_recv()

    landed(1, 0, 1)

    def four(k, carry):
        @pl.when(k > 0)
        def _():
            landed(2 * k, 0, 2 * k)
            landed(2 * k + 1, 0, 2 * k + 1)

        blocks([(2 * k, 0), (2 * k, 1), (2 * k + 1, 0), (2 * k + 1, 1)])
        return carry

    lax.fori_loop(0, 3, four, 0)
    landed(6, 1, 6)
    landed(7, 1, 7)
    landed(6, 2, 8)
    landed(7, 2, 9)
    blocks([(6, 0), (6, 1), (7, 0), (7, 1)])
    pack(1)
    partials1 = start(partial_copies(1))
    loads[8].wait()
    arrived(partials0)
    finish(0)
    arrived(partials1)
    finish(1)
    for copy in group_copies + sent + partials0 + partials1:
        copy.wait_send()


def body(q_nope, q_rope, w_absorb, w_value, cache, res_len, prefill_rows, block_dest, new_rows):
    rows = 4 * PART
    out = pl.pallas_call(
        kernel,
        out_shape=jax.ShapeDtypeStruct((rows, 128), BF16),
        in_specs=[pl.BlockSpec(memory_space=pl.ANY)] * 9,
        out_specs=pl.BlockSpec(memory_space=pltpu.VMEM),
        scratch_shapes=[
            pltpu.VMEM((rows, 128), BF16),
            pltpu.VMEM((rows, ROPE), BF16),
            pltpu.SMEM(res_len.shape, jnp.int32),
            pltpu.SMEM(block_dest.shape, jnp.int32),
            pltpu.VMEM((STEPS, 4, ROW), BF16),
            pltpu.VMEM(w_absorb.shape, BF16),
            pltpu.VMEM(w_value.shape, BF16),
            pltpu.VMEM((2, ROW, CTX), BF16),
            pltpu.VMEM((8, ROW, BLK), BF16),
            pltpu.VMEM((7, KMSG, 128), BF16),
            pltpu.VMEM((8, KMSG, 128), BF16),
            pltpu.VMEM((2, NZ, NX, QMSG, 128), BF16),
            pltpu.VMEM((4, QROWS, LAT + 128), BF16),
            pltpu.VMEM((2, QROWS, CTX), F32),
            pltpu.VMEM((2, QROWS, CTX), BF16),
            pltpu.VMEM((4, QROWS, LAT), F32),
            pltpu.VMEM((4, QROWS, 128), F32),
            pltpu.VMEM((4, QROWS, 128), F32),
            pltpu.VMEM((32, LAT + ROPE), F32),
            pltpu.VMEM((rows, LAT), F32),
            pltpu.VMEM((rows, 128), F32),
            pltpu.VMEM((rows, 128), F32),
            pltpu.VMEM((2, NSEQ, PMSG, 128), BF16),
            pltpu.VMEM((2, NSEQ, PMSG, 128), BF16),
            pltpu.SemaphoreType.DMA((9,)),
            pltpu.SemaphoreType.DMA((9,)),
            pltpu.SemaphoreType.DMA((10,)),
            pltpu.SemaphoreType.DMA((2, 12)),
            pltpu.SemaphoreType.DMA((2, 12)),
            pltpu.SemaphoreType.DMA((2, 6)),
            pltpu.SemaphoreType.DMA((2, 6)),
            pltpu.SemaphoreType.DMA((2, NSEQ)),
            pltpu.SemaphoreType.DMA((2, NSEQ)),
        ],
        compiler_params=pltpu.CompilerParams(
            collective_id=0, has_side_effects=True, vmem_limit_bytes=56 * 1024 * 1024
        ),
        name="latent_attention",
    )(
        q_nope.reshape(rows, 128),
        q_rope.reshape(rows, ROPE),
        w_absorb,
        w_value,
        cache.transpose(0, 2, 1),
        res_len,
        prefill_rows.transpose(0, 1, 3, 2),
        block_dest,
        new_rows.transpose(1, 0, 2),
    )
    return out.reshape(q_nope.shape)


def solution(mesh):
    in_specs = (
        P("group", None, "seq", None),
        P("group", None, "seq", None),
        P("seq", None, None),
        P("seq", None, None),
        P("group", "seq", None),
        P("group"),
        P("group", "seq", None, None),
        P("group", "seq"),
        P("group", None, None),
    )
    out_specs = P("group", None, "seq", None)
    return jax.shard_map(body, mesh=mesh, in_specs=in_specs, out_specs=out_specs, check_vma=False)
```

```python
import functools
import math

import jax
import jax.numpy as jnp
from jax import lax
from jax.experimental import pallas as pl
from jax.experimental.pallas import tpu as pltpu
from jax.sharding import PartitionSpec as P

MESH = pl.DeviceIdType.MESH
F32 = jnp.float32
BF16 = jnp.bfloat16

NY, NC, NZ, NX = 4, 2, 4, 4
HEADS = 8
STEPS = 3
PART = STEPS * HEADS
ROWS = 2 * PART
NSEQ = NZ * NX
QROWS = NSEQ * PART
LAT, ROPE = 512, 64
BLK = 128
CTX = 2048
QMSG = 4 * ROWS + 32
QCUT = QMSG // 2
PMSG = 4 * ROWS + 16
ROW = LAT + ROPE
KMSG = 16 + 2 * ROW
NEG = -1e30
EXPC = (128 + 64) ** -0.5 * math.log2(math.e)

ALONG_Y = (1, 3, 2)
FAR_FIRST = [
    (1, 2), (2, 1), (3, 2), (2, 3), (2, 2), (1, 1), (3, 3), (1, 3), (3, 1), (0, 2), (2, 0), (0, 1), (1, 0), (0, 3), (3, 0),
]


def dot_t(a, b):
    return lax.dot_general(a, b, (((1,), (1,)), ((), ())), preferred_element_type=F32)


def dot(a, b):
    return jnp.dot(a, b, preferred_element_type=F32)


def kernel(
    qn_hbm, qr_hbm, wa_hbm, wv_hbm, cache_hbm, len_hbm, pre_hbm, dest_hbm, new_hbm,
    out_ref,
    qn_ref, qr_ref, len_ref, dest_ref, new_ref, wa, wv, cache, pre, ysend, kv, qbuf, qall, scores, weights, acc, peak, total,
    fresh, fresh_w, fresh_m, fresh_l, pout, pin,
    local_sem, y_ss, y_rs, a_ss, a_rs, f_ss, f_rs, p_ss, p_rs,
):
    g, s = lax.axis_index("group"), lax.axis_index("seq")
    y, c = lax.div(g, NC), lax.rem(g, NC)
    z, x = lax.div(s, NX), lax.rem(s, NX)

    def group_dev(dy, core):
        return (lax.rem(y + dy, NY) * NC + core, s)

    def seq_dev(dz, dx):
        return (g, lax.rem(z + dz, NZ) * NX + lax.rem(x + dx, NX))

    loads = [
        pltpu.make_async_copy(src, dst, local_sem.at[i])
        for i, (src, dst) in enumerate(
            [
                (dest_hbm, dest_ref), (pre_hbm.at[0], pre), (qn_hbm, qn_ref), (qr_hbm, qr_ref), (wa_hbm, wa),
                (new_hbm, new_ref), (len_hbm, len_ref), (cache_hbm, cache), (wv_hbm, wv),
            ]
        )
    ]
    barrier = pltpu.get_barrier_semaphore()
    for device in (
        [group_dev(dy, core) for dy in ALONG_Y for core in range(NC)]
        + [group_dev(0, 1 - c)]
        + [seq_dev(0, d) for d in (1, 2, 3)]
        + [seq_dev(d, 0) for d in (1, 2, 3)]
    ):
        pl.semaphore_signal(barrier, inc=1, device_id=device, device_id_type=MESH)

    for load in loads:
        load.start()

    def start(copies):
        for copy in copies:
            copy.start()
        return copies

    loads[0].wait()
    owners = [dest_ref[0, k] for k in range(8)]
    targets = [lax.div(o, 2) for o in owners]
    members = [lax.rem(o, 2) for o in owners]
    tag_row = lax.broadcasted_iota(jnp.int32, (16, 128), 0)

    def pick(to, wanted):
        first = second = jnp.int32(0)
        tag_first = tag_second = jnp.int32(2)
        for k in reversed(range(8)):
            match = targets[k] == wanted
            second = jnp.where(match, first, second)
            tag_second = jnp.where(match, tag_first, tag_second)
            first = jnp.where(match, k, first)
            tag_first = jnp.where(match, members[k], tag_first)
        for slot, index in enumerate((first, second)):
            to[pl.ds(16 + slot * ROW, ROW), :] = pre[index]
        tags = jnp.where(tag_row < 8, tag_first, tag_second)
        to[pl.ds(0, 16), :] = tags.astype(F32).astype(BF16)

    def core_copy():
        return pltpu.make_async_remote_copy(
            src_ref=ysend.at[6], dst_ref=kv.at[1], send_sem=y_ss.at[6], recv_sem=y_rs.at[1],
            device_id=group_dev(0, 1 - c), device_id_type=MESH,
        )

    parts = [pl.ds(0, KMSG), pl.ds(0, 16 + ROW), pl.ds(16 + ROW, ROW)]

    def y_copy(k, core, part):
        there = 2 + 2 * ALONG_Y.index((NY - ALONG_Y[k]) % NY) + c
        late = 2 if part == 2 else 0
        return pltpu.make_async_remote_copy(
            src_ref=ysend.at[3 * core + k, parts[part]], dst_ref=kv.at[there, parts[part]],
            send_sem=y_ss.at[3 * core + k + (5 - 2 * core if late else 0)], recv_sem=y_rs.at[there + late],
            device_id=group_dev(ALONG_Y[k], core), device_id_type=MESH,
        )

    def pick_for(core):
        for k in range(3):
            pick(ysend.at[3 * core + k], lax.rem(y + ALONG_Y[k], NY) * NC + core)

    def blocks_to(core):
        return start(
            [y_copy(k, core, part) for k in range(3) for part in (0,)]
        )

    loads[1].wait()
    pick_for(0)

    for load in loads[2:5]:
        load.wait()
    row = lax.broadcasted_iota(jnp.int32, (2 * ROWS, 128), 0)
    own = qn_ref[...].astype(F32)
    spread = [jnp.where((row & 7) == h, own, 0.0).astype(BF16) for h in range(HEADS)]
    q_latent = dot(jnp.concatenate(spread, axis=1), wa[...].reshape(HEADS * 128, LAT))
    q_latent = q_latent.astype(BF16)
    for pair in range(2):
        rows = slice(pair * ROWS, (pair + 1) * ROWS)
        for p in range(4):
            qbuf[pair, 0, 0, pl.ds(p * ROWS, ROWS), :] = q_latent[rows, p * 128 : (p + 1) * 128]
        ropes = [qr_ref[pl.ds(pair * ROWS + 16 * i, 16), :] for i in range(3)]
        ropes.append(jnp.zeros((16, ROPE), BF16))
        for i in range(2):
            qbuf[pair, 0, 0, pl.ds(4 * ROWS + 16 * i, 16), :] = jnp.concatenate(
                ropes[2 * i : 2 * i + 2], axis=1
            )

    pl.semaphore_wait(barrier, 2 * NY - 1 + 6)
    group_copies = blocks_to(0)

    low, high = pl.ds(0, QCUT), pl.ds(QCUT, QMSG - QCUT)

    def own_copy(pair, index, dz, dx, rows):
        return pltpu.make_async_remote_copy(
            src_ref=qbuf.at[pair, 0, 0, rows], dst_ref=qbuf.at[pair, (NZ - dz) % NZ, (NX - dx) % NX, rows],
            send_sem=a_ss.at[pair, index], recv_sem=a_rs.at[pair, index],
            device_id=seq_dev(dz, dx), device_id_type=MESH,
        )

    def x_first(pair):
        return [own_copy(pair, d - 1, 0, d, low) for d in (1, 2, 3)]

    def z_first(pair):
        return [own_copy(pair, 2 + d, d, 0, high) for d in (1, 2, 3)]

    def rest(pair):
        return [own_copy(pair, 5 + d, 0, d, high) for d in (1, 2, 3)] + [
            own_copy(pair, 8 + d, d, 0, low) for d in (1, 2, 3)
        ]

    def forward_z(pair):
        return [
            pltpu.make_async_remote_copy(
                src_ref=qbuf.at[pair, 0, pl.ds(1, 3), low], dst_ref=qbuf.at[pair, NZ - d, pl.ds(1, 3), low],
                send_sem=f_ss.at[pair, d - 1], recv_sem=f_rs.at[pair, d - 1],
                device_id=seq_dev(d, 0), device_id_type=MESH,
            )
            for d in (1, 2, 3)
        ]

    def forward_x(pair):
        return [
            pltpu.make_async_remote_copy(
                src_ref=qbuf.at[pair, pl.ds(1, 3), 0, high], dst_ref=qbuf.at[pair, pl.ds(1, 3), NX - d, high],
                send_sem=f_ss.at[pair, 2 + d], recv_sem=f_rs.at[pair, 2 + d],
                device_id=seq_dev(0, d), device_id_type=MESH,
            )
            for d in (1, 2, 3)
        ]

    def arrived(copies):
        for copy in copies:
            copy.wait_recv()

    first_x, first_z = start(x_first(0)), start(z_first(0))
    others = start(rest(0))
    first_x1, first_z1 = start(x_first(1)), start(z_first(1))
    arrived(first_x)
    forward_z0 = start(forward_z(0))
    arrived(first_z)
    forward_x0 = start(forward_x(0))
    others1 = start(rest(1))
    sent = first_x + first_z + others + first_x1 + first_z1 + others1
    arrived(first_x1)
    forward_z1 = start(forward_z(1))
    arrived(first_z1)
    forward_x1 = start(forward_x(1))
    sent += forward_z0 + forward_x0 + forward_z1 + forward_x1

    pick_for(1)
    group_copies += blocks_to(1)
    pick(ysend.at[6], y * NC + 1 - c)
    group_copies += start([core_copy()])
    pick(kv.at[0], y * NC + c)

    loads[5].wait()
    fresh[...] = jnp.zeros_like(fresh)
    for u in range(STEPS):
        new = new_ref[u].astype(F32)
        for r in range(4):
            fresh[pl.ds(8 * r + u, 1), :] = new[r : r + 1]
    fresh_rows = fresh[...].astype(BF16)
    s_fresh = dot_t(q_latent, fresh_rows[:, :LAT]) + dot_t(
        qr_ref[...], fresh_rows[:, LAT : LAT + ROPE]
    )
    part = lax.broadcasted_iota(jnp.int32, (2 * ROWS, 32), 0) >> 3
    key = lax.broadcasted_iota(jnp.int32, (2 * ROWS, 32), 1)
    request = (
        (part >= 3).astype(jnp.int32) + (part >= 6).astype(jnp.int32) + (part >= 9).astype(jnp.int32)
    )
    step = part - 3 * request
    allowed = ((key >> 3) == request) & ((key & 7) <= step)
    s_fresh = jnp.where(allowed, s_fresh, NEG)
    m_fresh = jnp.max(s_fresh, axis=1, keepdims=True)
    p_fresh = jnp.where(allowed, jnp.exp2((s_fresh - m_fresh) * EXPC), 0.0)
    fresh_m[...] = jnp.broadcast_to(m_fresh, fresh_m.shape)
    fresh_l[...] = jnp.broadcast_to(jnp.sum(p_fresh, axis=1, keepdims=True), fresh_l.shape)
    fresh_w[...] = dot(p_fresh.astype(BF16), fresh_rows[:, :LAT])

    def assemble(pair):
        def two(i, carry):
            at = pl.multiple_of(i * 2 * PART, 16)
            dz, dx = lax.div(i, 2), lax.rem(i, 2) * 2
            def part(d, p):
                if p < 4:
                    return qbuf[pair, dz, dx + d, pl.ds(p * ROWS, ROWS), :].astype(F32)
                first, second = (
                    qbuf[pair, dz, dx + d, pl.ds(4 * ROWS + 16 * i, 16), :].astype(F32) for i in range(2)
                )
                return jnp.concatenate([first, pltpu.roll(first, ROPE, 1), second], axis=0)

            for p in range(5):
                one, two = part(0, p), part(1, p)
                lanes = slice(p * 128, (p + 1) * 128)
                for r in range(2):
                    rows = slice(r * PART, (r + 1) * PART)
                    qall[2 * pair + r, pl.ds(at, 2 * PART), lanes] = jnp.concatenate(
                        [one[rows], two[rows]], axis=0
                    ).astype(BF16)
            return carry

        lax.fori_loop(0, NSEQ // 2, two, 0)

    def pack(pair):
        lane = lax.broadcasted_iota(jnp.int32, (16, 128), 1)

        def one(j, carry):
            at = pl.multiple_of(j * PART, 8)

            def both(ref):
                return jnp.concatenate(
                    [ref[2 * pair, pl.ds(at, PART), :], ref[2 * pair + 1, pl.ds(at, PART), :]], axis=0
                )

            for p in range(4):
                lanes = slice(p * 128, (p + 1) * 128)
                pout[pair, j, pl.ds(p * ROWS, ROWS), :] = jnp.concatenate(
                    [acc[2 * pair, pl.ds(at, PART), lanes], acc[2 * pair + 1, pl.ds(at, PART), lanes]],
                    axis=0,
                ).astype(BF16)
            m, l = both(peak), both(total)
            m_high = m.astype(BF16).astype(F32)
            m_mid = (m - m_high).astype(BF16).astype(F32)
            m_low = m - m_high - m_mid
            l_high = l.astype(BF16).astype(F32)
            stats = jnp.zeros((16, 128), F32)
            for i in range(3):
                rows = slice(16 * i, 16 * (i + 1))
                for q, value in enumerate((m_high, m_mid, m_low, l_high, l - l_high)):
                    stats = jnp.where(lane == 8 * i + q, value[rows], stats)
            pout[pair, j, pl.ds(4 * ROWS, 16), :] = stats.astype(BF16)
            return carry

        lax.fori_loop(0, NSEQ, one, 0)

    def partial_copy(pair, j):
        dz, dx = lax.div(j, NX), lax.rem(j, NX)
        there = lax.rem(NZ - dz, NZ) * NX + lax.rem(NX - dx, NX)
        return pltpu.make_async_remote_copy(
            src_ref=pout.at[pair, j], dst_ref=pin.at[pair, there],
            send_sem=p_ss.at[pair, j], recv_sem=p_rs.at[pair, there],
            device_id=seq_dev(dz, dx), device_id_type=MESH,
        )

    def partial_copies(pair):
        return [partial_copy(pair, dz * NX + dx) for dz, dx in FAR_FIRST]

    def finish(pair):
        stats = jnp.concatenate(
            [pout[pair, 0, pl.ds(4 * ROWS, 16), :]]
            + [pin[pair, j, pl.ds(4 * ROWS, 16), :] for j in range(1, NSEQ)],
            axis=0,
        )
        source = lax.broadcasted_iota(jnp.int32, (128, 128), 0)
        picks = [
            ((source >= 8 * i) & (source < 8 * i + 3)).astype(F32).astype(BF16) for i in range(3)
        ] + [
            ((source >= 8 * i + 3) & (source < 8 * i + 5)).astype(F32).astype(BF16) for i in range(3)
        ]
        spread_stats = dot(stats, jnp.concatenate(picks, axis=1))

        def of(j, kind):
            return jnp.concatenate(
                [
                    spread_stats[16 * j : 16 * (j + 1), 128 * (3 * kind + i) : 128 * (3 * kind + i + 1)]
                    for i in range(3)
                ],
                axis=0,
            )

        rows = pl.ds(pair * ROWS, ROWS)
        peaks = [of(j, 0) for j in range(NSEQ)]
        m_fresh = fresh_m[rows, :]
        top = m_fresh
        for m in peaks:
            top = jnp.maximum(top, m)
        keep = jnp.exp2((m_fresh - top) * EXPC)
        sums = keep * fresh_l[rows, :]
        values = [keep * fresh_w[rows, p * 128 : (p + 1) * 128] for p in range(4)]
        for j in range(NSEQ):
            keep = jnp.exp2((peaks[j] - top) * EXPC)
            sums = sums + keep * of(j, 1)
            message = pout if j == 0 else pin
            for p in range(4):
                values[p] = values[p] + keep * message[pair, j, pl.ds(p * ROWS, ROWS), :].astype(F32)
        head = lax.broadcasted_iota(jnp.int32, (ROWS, 128), 0) & 7
        attended = [(v / sums).astype(BF16).astype(F32) for v in values]
        spread = [
            jnp.where(head == h, attended[p], 0.0).astype(BF16) for h in range(HEADS) for p in range(4)
        ]
        result = dot(jnp.concatenate(spread, axis=1), wv[...].reshape(HEADS * LAT, 128))
        out_ref[rows, :] = result.astype(BF16)

    arrived(others + forward_z0 + forward_x0)
    assemble(0)
    loads[6].wait()
    loads[7].wait()

    tile = 512
    tiles = range(CTX // tile)
    position = lax.broadcasted_iota(jnp.int32, (QROWS, tile), 1)

    def score(r, k, running):
        keys = pl.ds(k * tile, tile)
        sc = dot(qall[r, :, :ROW], cache[r, :, keys])
        sc = jnp.where(position < len_ref[r] - s * CTX - k * tile, sc, NEG)
        scores[r, :, keys] = sc
        for i in range(tile // 128):
            running = jnp.maximum(running, sc[:, i * 128 : (i + 1) * 128])
        return running

    def weigh(r, k, m, sums):
        keys = pl.ds(k * tile, tile)
        w = jnp.exp2((scores[r, :, keys] - m) * EXPC)
        for i in range(tile // 128):
            sums = sums + w[:, i * 128 : (i + 1) * 128]
        weights[r, :, keys] = w.astype(BF16)
        return sums

    def done(r, m, sums):
        peak[r] = jnp.broadcast_to(m, (QROWS, 128))
        total[r] = jnp.broadcast_to(jnp.sum(sums, axis=1, keepdims=True), (QROWS, 128))

    lowest, nothing = jnp.full((QROWS, 128), NEG, F32), jnp.zeros((QROWS, 128), F32)
    m0 = m1 = lowest
    for k in tiles:
        m0 = score(0, k, m0)
    m0 = jnp.max(m0, axis=1, keepdims=True)
    sums0 = sums1 = nothing
    for k in tiles:
        m1 = score(1, k, m1)
        sums0 = weigh(0, k, m0, sums0)
    m1 = jnp.max(m1, axis=1, keepdims=True)
    done(0, m0, sums0)
    acc[0] = dot_t(weights[0], cache[0, :LAT, :])
    for k in tiles:
        sums1 = weigh(1, k, m1, sums1)
    done(1, m1, sums1)
    acc[1] = dot_t(weights[1], cache[1, :LAT, :])
    pack(0)
    partials0 = start(partial_copies(0))

    arrived(others1 + forward_z1 + forward_x1)
    assemble(1)
    for r in (2, 3):
        acc[r] = jnp.zeros((QROWS, LAT), F32)
        peak[r] = jnp.full((QROWS, 128), NEG, F32)
        total[r] = jnp.zeros((QROWS, 128), F32)

    def blocks(taken):
        keys = jnp.concatenate([kv[i, pl.ds(16 + slot * ROW, ROW), :] for i, slot in taken], axis=1)
        tag = jnp.concatenate(
            [kv[i, pl.ds(0, 16), :].astype(F32)[8 * slot : 8 * slot + 1] for i, slot in taken], axis=1
        )
        count = len(taken)
        new = (2, 3)
        scs = [jnp.where(tag == float(r - 2), dot(qall[r, :, :ROW], keys), NEG) for r in new]
        pieces = [[sc[:, n * 128 : (n + 1) * 128] for n in range(count)] for sc in scs]
        olds = [peak[r] for r in new]
        tops = [
            jnp.maximum(old, jnp.max(functools.reduce(jnp.maximum, some), axis=1, keepdims=True))
            for old, some in zip(olds, pieces)
        ]
        ws = [[jnp.exp2((piece - top) * EXPC) for piece in some] for some, top in zip(pieces, tops)]
        terms = [dot_t(jnp.concatenate(w, axis=1).astype(BF16), keys[:LAT]) for w in ws]
        for r, old, top, w, term in zip(new, olds, tops, ws, terms):
            keep = jnp.exp2((old - top) * EXPC)
            peak[r] = top
            total[r] = total[r] * keep + jnp.sum(sum(w[1:], w[0]), axis=1, keepdims=True)
            for p in range(4):
                lanes = slice(p * 128, (p + 1) * 128)
                acc[r, :, lanes] = acc[r, :, lanes] * keep + term[:, lanes]

    def landed(i, part, sem):
        pltpu.make_async_remote_copy(
            src_ref=ysend.at[6, parts[part]], dst_ref=kv.at[i, parts[part]],
            send_sem=y_ss.at[6], recv_sem=y_rs.at[sem],
            device_id=group_dev(0, 1 - c), device_id_type=MESH,
        ).wait_recv()

    landed(1, 0, 1)

    def four(k, carry):
        @pl.when(k > 0)
        def _():
            landed(2 * k, 0, 2 * k)
            landed(2 * k + 1, 0, 2 * k + 1)

        blocks([(2 * k, 0), (2 * k, 1), (2 * k + 1, 0), (2 * k + 1, 1)])
        return carry

    lax.fori_loop(0, 4, four, 0)
    pack(1)
    partials1 = start(partial_copies(1))
    loads[8].wait()
    arrived(partials0)
    finish(0)
    arrived(partials1)
    finish(1)
    for copy in group_copies + sent + partials0 + partials1:
        copy.wait_send()


def body(q_nope, q_rope, w_absorb, w_value, cache, res_len, prefill_rows, block_dest, new_rows):
    rows = 4 * PART
    out = pl.pallas_call(
        kernel,
        out_shape=jax.ShapeDtypeStruct((rows, 128), BF16),
        in_specs=[pl.BlockSpec(memory_space=pl.ANY)] * 9,
        out_specs=pl.BlockSpec(memory_space=pltpu.VMEM),
        scratch_shapes=[
            pltpu.VMEM((rows, 128), BF16),
            pltpu.VMEM((rows, ROPE), BF16),
            pltpu.SMEM(res_len.shape, jnp.int32),
            pltpu.SMEM(block_dest.shape, jnp.int32),
            pltpu.VMEM((STEPS, 4, ROW), BF16),
            pltpu.VMEM(w_absorb.shape, BF16),
            pltpu.VMEM(w_value.shape, BF16),
            pltpu.VMEM((2, ROW, CTX), BF16),
            pltpu.VMEM((8, ROW, BLK), BF16),
            pltpu.VMEM((7, KMSG, 128), BF16),
            pltpu.VMEM((8, KMSG, 128), BF16),
            pltpu.VMEM((2, NZ, NX, QMSG, 128), BF16),
            pltpu.VMEM((4, QROWS, LAT + 128), BF16),
            pltpu.VMEM((2, QROWS, CTX), F32),
            pltpu.VMEM((2, QROWS, CTX), BF16),
            pltpu.VMEM((4, QROWS, LAT), F32),
            pltpu.VMEM((4, QROWS, 128), F32),
            pltpu.VMEM((4, QROWS, 128), F32),
            pltpu.VMEM((32, LAT + ROPE), F32),
            pltpu.VMEM((rows, LAT), F32),
            pltpu.VMEM((rows, 128), F32),
            pltpu.VMEM((rows, 128), F32),
            pltpu.VMEM((2, NSEQ, PMSG, 128), BF16),
            pltpu.VMEM((2, NSEQ, PMSG, 128), BF16),
            pltpu.SemaphoreType.DMA((9,)),
            pltpu.SemaphoreType.DMA((9,)),
            pltpu.SemaphoreType.DMA((10,)),
            pltpu.SemaphoreType.DMA((2, 12)),
            pltpu.SemaphoreType.DMA((2, 12)),
            pltpu.SemaphoreType.DMA((2, 6)),
            pltpu.SemaphoreType.DMA((2, 6)),
            pltpu.SemaphoreType.DMA((2, NSEQ)),
            pltpu.SemaphoreType.DMA((2, NSEQ)),
        ],
        compiler_params=pltpu.CompilerParams(
            collective_id=0, has_side_effects=True, vmem_limit_bytes=56 * 1024 * 1024
        ),
        name="latent_attention",
    )(
        q_nope.reshape(rows, 128),
        q_rope.reshape(rows, ROPE),
        w_absorb,
        w_value,
        cache.transpose(0, 2, 1),
        res_len,
        prefill_rows.transpose(0, 1, 3, 2),
        block_dest,
        new_rows.transpose(1, 0, 2),
    )
    return out.reshape(q_nope.shape)


def solution(mesh):
    in_specs = (
        P("group", None, "seq", None),
        P("group", None, "seq", None),
        P("seq", None, None),
        P("seq", None, None),
        P("group", "seq", None),
        P("group"),
        P("group", "seq", None, None),
        P("group", "seq"),
        P("group", None, None),
    )
    out_specs = P("group", None, "seq", None)
    return jax.shard_map(body, mesh=mesh, in_specs=in_specs, out_specs=out_specs, check_vma=False)
```

```python
import functools
import math

import jax
import jax.numpy as jnp
from jax import lax
from jax.experimental import pallas as pl
from jax.experimental.pallas import tpu as pltpu
from jax.sharding import PartitionSpec as P

MESH = pl.DeviceIdType.MESH
F32 = jnp.float32
BF16 = jnp.bfloat16

NY, NC, NZ, NX = 4, 2, 4, 4
HEADS = 8
STEPS = 3
PART = STEPS * HEADS
ROWS = 2 * PART
NSEQ = NZ * NX
QROWS = NSEQ * PART
LAT, ROPE = 512, 64
BLK = 128
CTX = 2048
QMSG = 4 * ROWS + 32
QCUT = QMSG // 2
PMSG = 4 * ROWS + 16
ROW = LAT + ROPE
KMSG = 16 + 2 * ROW
NEG = -1e30
EXPC = (128 + 64) ** -0.5 * math.log2(math.e)

ALONG_Y = (1, 3, 2)
FAR_FIRST = [
    (1, 2), (2, 1), (3, 2), (2, 3), (2, 2), (1, 1), (3, 3), (1, 3), (3, 1), (0, 2), (2, 0), (0, 1), (1, 0), (0, 3), (3, 0),
]


def dot_t(a, b):
    return lax.dot_general(a, b, (((1,), (1,)), ((), ())), preferred_element_type=F32)


def dot(a, b):
    return jnp.dot(a, b, preferred_element_type=F32)


def kernel(
    qn_hbm, qr_hbm, wa_hbm, wv_hbm, cache_hbm, len_hbm, pre_hbm, dest_hbm, new_hbm,
    out_ref,
    qn_ref, qr_ref, len_ref, dest_ref, new_ref, wa, wv, cache, pre, ysend, kv, qbuf, qall, scores, weights, acc, peak, total,
    fresh, fresh_w, fresh_m, fresh_l, pout, pin,
    local_sem, y_ss, y_rs, a_ss, a_rs, f_ss, f_rs, p_ss, p_rs,
):
    g, s = lax.axis_index("group"), lax.axis_index("seq")
    y, c = lax.div(g, NC), lax.rem(g, NC)
    z, x = lax.div(s, NX), lax.rem(s, NX)

    def group_dev(dy, core):
        return (lax.rem(y + dy, NY) * NC + core, s)

    def seq_dev(dz, dx):
        return (g, lax.rem(z + dz, NZ) * NX + lax.rem(x + dx, NX))

    loads = [
        pltpu.make_async_copy(src, dst, local_sem.at[i])
        for i, (src, dst) in enumerate(
            [
                (dest_hbm, dest_ref), (pre_hbm.at[0], pre), (qn_hbm, qn_ref), (qr_hbm, qr_ref), (wa_hbm, wa),
                (new_hbm, new_ref), (len_hbm, len_ref), (cache_hbm, cache), (wv_hbm, wv),
            ]
        )
    ]
    barrier = pltpu.get_barrier_semaphore()
    for device in (
        [group_dev(dy, core) for dy in ALONG_Y for core in range(NC)]
        + [group_dev(0, 1 - c)]
        + [seq_dev(0, d) for d in (1, 2, 3)]
        + [seq_dev(d, 0) for d in (1, 2, 3)]
    ):
        pl.semaphore_signal(barrier, inc=1, device_id=device, device_id_type=MESH)

    for load in loads:
        load.start()

    def start(copies):
        for copy in copies:
            copy.start()
        return copies

    loads[0].wait()
    owners = [dest_ref[0, k] for k in range(8)]
    targets = [lax.div(o, 2) for o in owners]
    members = [lax.rem(o, 2) for o in owners]
    tag_row = lax.broadcasted_iota(jnp.int32, (16, 128), 0)

    def pick(to, wanted):
        first = second = jnp.int32(0)
        tag_first = tag_second = jnp.int32(2)
        for k in reversed(range(8)):
            match = targets[k] == wanted
            second = jnp.where(match, first, second)
            tag_second = jnp.where(match, tag_first, tag_second)
            first = jnp.where(match, k, first)
            tag_first = jnp.where(match, members[k], tag_first)
        for slot, index in enumerate((first, second)):
            to[pl.ds(16 + slot * ROW, ROW), :] = pre[index]
        tags = jnp.where(tag_row < 8, tag_first, tag_second)
        to[pl.ds(0, 16), :] = tags.astype(F32).astype(BF16)

    def core_copy():
        return pltpu.make_async_remote_copy(
            src_ref=ysend.at[6], dst_ref=kv.at[1], send_sem=y_ss.at[6], recv_sem=y_rs.at[1],
            device_id=group_dev(0, 1 - c), device_id_type=MESH,
        )

    parts = [pl.ds(0, KMSG), pl.ds(0, 16 + ROW), pl.ds(16 + ROW, ROW)]

    def y_copy(k, core, part):
        there = 2 + 2 * ALONG_Y.index((NY - ALONG_Y[k]) % NY) + c
        late = 2 if part == 2 else 0
        return pltpu.make_async_remote_copy(
            src_ref=ysend.at[3 * core + k, parts[part]], dst_ref=kv.at[there, parts[part]],
            send_sem=y_ss.at[3 * core + k + (5 - 2 * core if late else 0)], recv_sem=y_rs.at[there + late],
            device_id=group_dev(ALONG_Y[k], core), device_id_type=MESH,
        )

    def pick_for(core):
        for k in range(3):
            pick(ysend.at[3 * core + k], lax.rem(y + ALONG_Y[k], NY) * NC + core)

    def blocks_to(core):
        return start(
            [y_copy(k, core, part) for k in range(3) for part in (0,)]
        )

    loads[1].wait()
    pick_for(1)

    pl.semaphore_wait(barrier, 2 * NY - 1 + 6)
    group_copies = blocks_to(1)

    for load in loads[2:5]:
        load.wait()
    row = lax.broadcasted_iota(jnp.int32, (2 * ROWS, 128), 0)
    own = qn_ref[...].astype(F32)
    spread = [jnp.where((row & 7) == h, own, 0.0).astype(BF16) for h in range(HEADS)]
    q_latent = dot(jnp.concatenate(spread, axis=1), wa[...].reshape(HEADS * 128, LAT))
    q_latent = q_latent.astype(BF16)
    for pair in range(2):
        rows = slice(pair * ROWS, (pair + 1) * ROWS)
        for p in range(4):
            qbuf[pair, 0, 0, pl.ds(p * ROWS, ROWS), :] = q_latent[rows, p * 128 : (p + 1) * 128]
        ropes = [qr_ref[pl.ds(pair * ROWS + 16 * i, 16), :] for i in range(3)]
        ropes.append(jnp.zeros((16, ROPE), BF16))
        for i in range(2):
            qbuf[pair, 0, 0, pl.ds(4 * ROWS + 16 * i, 16), :] = jnp.concatenate(
                ropes[2 * i : 2 * i + 2], axis=1
            )

    low, high = pl.ds(0, QCUT), pl.ds(QCUT, QMSG - QCUT)

    def own_copy(pair, index, dz, dx, rows):
        return pltpu.make_async_remote_copy(
            src_ref=qbuf.at[pair, 0, 0, rows], dst_ref=qbuf.at[pair, (NZ - dz) % NZ, (NX - dx) % NX, rows],
            send_sem=a_ss.at[pair, index], recv_sem=a_rs.at[pair, index],
            device_id=seq_dev(dz, dx), device_id_type=MESH,
        )

    def x_first(pair):
        return [own_copy(pair, d - 1, 0, d, low) for d in (1, 2, 3)]

    def z_first(pair):
        return [own_copy(pair, 2 + d, d, 0, high) for d in (1, 2, 3)]

    def rest(pair):
        return [own_copy(pair, 5 + d, 0, d, high) for d in (1, 2, 3)] + [
            own_copy(pair, 8 + d, d, 0, low) for d in (1, 2, 3)
        ]

    def forward_z(pair):
        return [
            pltpu.make_async_remote_copy(
                src_ref=qbuf.at[pair, 0, pl.ds(1, 3), low], dst_ref=qbuf.at[pair, NZ - d, pl.ds(1, 3), low],
                send_sem=f_ss.at[pair, d - 1], recv_sem=f_rs.at[pair, d - 1],
                device_id=seq_dev(d, 0), device_id_type=MESH,
            )
            for d in (1, 2, 3)
        ]

    def forward_x(pair):
        return [
            pltpu.make_async_remote_copy(
                src_ref=qbuf.at[pair, pl.ds(1, 3), 0, high], dst_ref=qbuf.at[pair, pl.ds(1, 3), NX - d, high],
                send_sem=f_ss.at[pair, 2 + d], recv_sem=f_rs.at[pair, 2 + d],
                device_id=seq_dev(0, d), device_id_type=MESH,
            )
            for d in (1, 2, 3)
        ]

    def arrived(copies):
        for copy in copies:
            copy.wait_recv()

    first_x, first_z = start(x_first(0)), start(z_first(0))
    others = start(rest(0))
    first_x1, first_z1 = start(x_first(1)), start(z_first(1))
    arrived(first_x)
    forward_z0 = start(forward_z(0))
    arrived(first_z)
    forward_x0 = start(forward_x(0))
    others1 = start(rest(1))
    sent = first_x + first_z + others + first_x1 + first_z1 + others1
    arrived(first_x1)
    forward_z1 = start(forward_z(1))
    arrived(first_z1)
    forward_x1 = start(forward_x(1))
    sent += forward_z0 + forward_x0 + forward_z1 + forward_x1

    pick_for(0)
    group_copies += blocks_to(0)
    pick(ysend.at[6], y * NC + 1 - c)
    group_copies += start([core_copy()])
    pick(kv.at[0], y * NC + c)

    loads[5].wait()
    fresh[...] = jnp.zeros_like(fresh)
    for u in range(STEPS):
        new = new_ref[u].astype(F32)
        for r in range(4):
            fresh[pl.ds(8 * r + u, 1), :] = new[r : r + 1]
    fresh_rows = fresh[...].astype(BF16)
    s_fresh = dot_t(q_latent, fresh_rows[:, :LAT]) + dot_t(
        qr_ref[...], fresh_rows[:, LAT : LAT + ROPE]
    )
    part = lax.broadcasted_iota(jnp.int32, (2 * ROWS, 32), 0) >> 3
    key = lax.broadcasted_iota(jnp.int32, (2 * ROWS, 32), 1)
    request = (
        (part >= 3).astype(jnp.int32) + (part >= 6).astype(jnp.int32) + (part >= 9).astype(jnp.int32)
    )
    step = part - 3 * request
    allowed = ((key >> 3) == request) & ((key & 7) <= step)
    s_fresh = jnp.where(allowed, s_fresh, NEG)
    m_fresh = jnp.max(s_fresh, axis=1, keepdims=True)
    p_fresh = jnp.where(allowed, jnp.exp2((s_fresh - m_fresh) * EXPC), 0.0)
    fresh_m[...] = jnp.broadcast_to(m_fresh, fresh_m.shape)
    fresh_l[...] = jnp.broadcast_to(jnp.sum(p_fresh, axis=1, keepdims=True), fresh_l.shape)
    fresh_w[...] = dot(p_fresh.astype(BF16), fresh_rows[:, :LAT])

    def assemble(pair):
        def two(i, carry):
            at = pl.multiple_of(i * 2 * PART, 16)
            dz, dx = lax.div(i, 2), lax.rem(i, 2) * 2
            def part(d, p):
                if p < 4:
                    return qbuf[pair, dz, dx + d, pl.ds(p * ROWS, ROWS), :].astype(F32)
                first, second = (
                    qbuf[pair, dz, dx + d, pl.ds(4 * ROWS + 16 * i, 16), :].astype(F32) for i in range(2)
                )
                return jnp.concatenate([first, pltpu.roll(first, ROPE, 1), second], axis=0)

            for p in range(5):
                one, two = part(0, p), part(1, p)
                lanes = slice(p * 128, (p + 1) * 128)
                for r in range(2):
                    rows = slice(r * PART, (r + 1) * PART)
                    qall[2 * pair + r, pl.ds(at, 2 * PART), lanes] = jnp.concatenate(
                        [one[rows], two[rows]], axis=0
                    ).astype(BF16)
            return carry

        lax.fori_loop(0, NSEQ // 2, two, 0)

    def message(pair, j, lane, sums, peaks, totals):
        for p in range(4):
            lanes = slice(p * 128, (p + 1) * 128)
            pout[pair, j, pl.ds(p * ROWS, ROWS), :] = jnp.concatenate(
                [part[:, lanes] for part in sums], axis=0
            ).astype(BF16)
        m, l = jnp.concatenate(peaks, axis=0), jnp.concatenate(totals, axis=0)
        m_high = m.astype(BF16).astype(F32)
        m_mid = (m - m_high).astype(BF16).astype(F32)
        m_low = m - m_high - m_mid
        l_high = l.astype(BF16).astype(F32)
        stats = jnp.zeros((16, 128), F32)
        for i in range(3):
            rows = slice(16 * i, 16 * (i + 1))
            for q, value in enumerate((m_high, m_mid, m_low, l_high, l - l_high)):
                stats = jnp.where(lane == 8 * i + q, value[rows], stats)
        pout[pair, j, pl.ds(4 * ROWS, 16), :] = stats.astype(BF16)

    def pack(pair):
        lane = lax.broadcasted_iota(jnp.int32, (16, 128), 1)

        def one(j, carry):
            rows = pl.ds(pl.multiple_of(j * PART, 8), PART)
            message(
                pair, j, lane, *([ref[2 * pair + r, rows, :] for r in range(2)] for ref in (acc, peak, total))
            )
            return carry

        lax.fori_loop(0, NSEQ, one, 0)

    def partial_copy(pair, j):
        dz, dx = lax.div(j, NX), lax.rem(j, NX)
        there = lax.rem(NZ - dz, NZ) * NX + lax.rem(NX - dx, NX)
        return pltpu.make_async_remote_copy(
            src_ref=pout.at[pair, j], dst_ref=pin.at[pair, there],
            send_sem=p_ss.at[pair, j], recv_sem=p_rs.at[pair, there],
            device_id=seq_dev(dz, dx), device_id_type=MESH,
        )

    def partial_copies(pair):
        return [partial_copy(pair, dz * NX + dx) for dz, dx in FAR_FIRST]

    def finish(pair):
        stats = jnp.concatenate(
            [pout[pair, 0, pl.ds(4 * ROWS, 16), :]]
            + [pin[pair, j, pl.ds(4 * ROWS, 16), :] for j in range(1, NSEQ)],
            axis=0,
        )
        source = lax.broadcasted_iota(jnp.int32, (128, 128), 0)
        picks = [
            ((source >= 8 * i) & (source < 8 * i + 3)).astype(F32).astype(BF16) for i in range(3)
        ] + [
            ((source >= 8 * i + 3) & (source < 8 * i + 5)).astype(F32).astype(BF16) for i in range(3)
        ]
        spread_stats = dot(stats, jnp.concatenate(picks, axis=1))

        def of(j, kind):
            return jnp.concatenate(
                [
                    spread_stats[16 * j : 16 * (j + 1), 128 * (3 * kind + i) : 128 * (3 * kind + i + 1)]
                    for i in range(3)
                ],
                axis=0,
            )

        rows = pl.ds(pair * ROWS, ROWS)
        peaks = [of(j, 0) for j in range(NSEQ)]
        m_fresh = fresh_m[rows, :]
        top = m_fresh
        for m in peaks:
            top = jnp.maximum(top, m)
        keep = jnp.exp2((m_fresh - top) * EXPC)
        sums = keep * fresh_l[rows, :]
        values = [keep * fresh_w[rows, p * 128 : (p + 1) * 128] for p in range(4)]
        for j in range(NSEQ):
            keep = jnp.exp2((peaks[j] - top) * EXPC)
            sums = sums + keep * of(j, 1)
            message = pout if j == 0 else pin
            for p in range(4):
                values[p] = values[p] + keep * message[pair, j, pl.ds(p * ROWS, ROWS), :].astype(F32)
        head = lax.broadcasted_iota(jnp.int32, (ROWS, 128), 0) & 7
        attended = [(v / sums).astype(BF16).astype(F32) for v in values]
        spread = [
            jnp.where(head == h, attended[p], 0.0).astype(BF16) for h in range(HEADS) for p in range(4)
        ]
        result = dot(jnp.concatenate(spread, axis=1), wv[...].reshape(HEADS * LAT, 128))
        out_ref[rows, :] = result.astype(BF16)

    arrived(others + forward_z0 + forward_x0)
    assemble(0)
    loads[6].wait()
    loads[7].wait()

    tile = 512
    tiles = range(CTX // tile)
    position = lax.broadcasted_iota(jnp.int32, (QROWS, tile), 1)

    def score(r, k, running):
        keys = pl.ds(k * tile, tile)
        sc = dot(qall[r, :, :ROW], cache[r, :, keys])
        sc = jnp.where(position < len_ref[r] - s * CTX - k * tile, sc, NEG)
        scores[r, :, keys] = sc
        for i in range(tile // 128):
            running = jnp.maximum(running, sc[:, i * 128 : (i + 1) * 128])
        return running

    def weigh(r, k, m, sums):
        keys = pl.ds(k * tile, tile)
        w = jnp.exp2((scores[r, :, keys] - m) * EXPC)
        for i in range(tile // 128):
            sums = sums + w[:, i * 128 : (i + 1) * 128]
        weights[r, :, keys] = w.astype(BF16)
        return sums

    def done(r, m, sums):
        peak[r] = jnp.broadcast_to(m, (QROWS, 128))
        total[r] = jnp.broadcast_to(jnp.sum(sums, axis=1, keepdims=True), (QROWS, 128))

    lowest, nothing = jnp.full((QROWS, 128), NEG, F32), jnp.zeros((QROWS, 128), F32)
    m0 = m1 = lowest
    for k in tiles:
        m0 = score(0, k, m0)
    m0 = jnp.max(m0, axis=1, keepdims=True)
    sums0 = sums1 = nothing
    for k in tiles:
        m1 = score(1, k, m1)
        sums0 = weigh(0, k, m0, sums0)
    m1 = jnp.max(m1, axis=1, keepdims=True)
    done(0, m0, sums0)
    acc[0] = dot_t(weights[0], cache[0, :LAT, :])
    for k in tiles:
        sums1 = weigh(1, k, m1, sums1)
    done(1, m1, sums1)
    acc[1] = dot_t(weights[1], cache[1, :LAT, :])
    pack(0)
    partials0 = start(partial_copies(0))

    arrived(others1 + forward_z1 + forward_x1)
    assemble(1)
    for r in (2, 3):
        acc[r] = jnp.zeros((QROWS, LAT), F32)
        peak[r] = jnp.full((QROWS, 128), NEG, F32)
        total[r] = jnp.zeros((QROWS, 128), F32)

    def blocks(taken, last=False):
        keys = jnp.concatenate([kv[i, pl.ds(16 + slot * ROW, ROW), :] for i, slot in taken], axis=1)
        tag = jnp.concatenate(
            [kv[i, pl.ds(0, 16), :].astype(F32)[8 * slot : 8 * slot + 1] for i, slot in taken], axis=1
        )
        count = len(taken)
        new = (2, 3)
        scs = [jnp.where(tag == float(r - 2), dot(qall[r, :, :ROW], keys), NEG) for r in new]
        pieces = [[sc[:, n * 128 : (n + 1) * 128] for n in range(count)] for sc in scs]
        olds = [peak[r] for r in new]
        tops = [
            jnp.maximum(old, jnp.max(functools.reduce(jnp.maximum, some), axis=1, keepdims=True))
            for old, some in zip(olds, pieces)
        ]
        ws = [[jnp.exp2((piece - top) * EXPC) for piece in some] for some, top in zip(pieces, tops)]
        terms = [dot_t(jnp.concatenate(w, axis=1).astype(BF16), keys[:LAT]) for w in ws]
        keeps = [jnp.exp2((old - top) * EXPC) for old, top in zip(olds, tops)]
        totals = [
            total[r] * keep + jnp.sum(sum(w[1:], w[0]), axis=1, keepdims=True)
            for r, keep, w in zip(new, keeps, ws)
        ]
        four = [slice(p * 128, (p + 1) * 128) for p in range(4)]
        if last:
            lane = lax.broadcasted_iota(jnp.int32, (16, 128), 1)
            for dz, dx in FAR_FIRST + [(0, 0)]:
                j = dz * NX + dx
                rows = slice(j * PART, (j + 1) * PART)
                sums = [
                    jnp.concatenate(
                        [acc[r, rows, lanes] * keep[rows] + term[rows, lanes] for lanes in four], axis=1
                    )
                    for r, keep, term in zip(new, keeps, terms)
                ]
                message(1, j, lane, sums, [top[rows] for top in tops], [t[rows] for t in totals])
                if j > 0:
                    partial_copy(1, j).start()
            return
        for r, keep, top, sums, term in zip(new, keeps, tops, totals, terms):
            peak[r] = top
            total[r] = sums
            for lanes in four:
                acc[r, :, lanes] = acc[r, :, lanes] * keep + term[:, lanes]

    def landed(i, part, sem):
        pltpu.make_async_remote_copy(
            src_ref=ysend.at[6, parts[part]], dst_ref=kv.at[i, parts[part]],
            send_sem=y_ss.at[6], recv_sem=y_rs.at[sem],
            device_id=group_dev(0, 1 - c), device_id_type=MESH,
        ).wait_recv()

    landed(1, 0, 1)

    def four(k, carry):
        @pl.when(k > 0)
        def _():
            landed(2 * k, 0, 2 * k)
            landed(2 * k + 1, 0, 2 * k + 1)

        blocks([(2 * k, 0), (2 * k, 1), (2 * k + 1, 0), (2 * k + 1, 1)])
        return carry

    lax.fori_loop(0, 3, four, 0)
    landed(6, 0, 6)
    landed(7, 0, 7)
    blocks([(6, 0), (6, 1), (7, 0), (7, 1)], last=True)
    partials1 = partial_copies(1)
    loads[8].wait()
    arrived(partials0)
    finish(0)
    arrived(partials1)
    finish(1)
    for copy in group_copies + sent + partials0 + partials1:
        copy.wait_send()


def body(q_nope, q_rope, w_absorb, w_value, cache, res_len, prefill_rows, block_dest, new_rows):
    rows = 4 * PART
    out = pl.pallas_call(
        kernel,
        out_shape=jax.ShapeDtypeStruct((rows, 128), BF16),
        in_specs=[pl.BlockSpec(memory_space=pl.ANY)] * 9,
        out_specs=pl.BlockSpec(memory_space=pltpu.VMEM),
        scratch_shapes=[
            pltpu.VMEM((rows, 128), BF16),
            pltpu.VMEM((rows, ROPE), BF16),
            pltpu.SMEM(res_len.shape, jnp.int32),
            pltpu.SMEM(block_dest.shape, jnp.int32),
            pltpu.VMEM((STEPS, 4, ROW), BF16),
            pltpu.VMEM(w_absorb.shape, BF16),
            pltpu.VMEM(w_value.shape, BF16),
            pltpu.VMEM((2, ROW, CTX), BF16),
            pltpu.VMEM((8, ROW, BLK), BF16),
            pltpu.VMEM((7, KMSG, 128), BF16),
            pltpu.VMEM((8, KMSG, 128), BF16),
            pltpu.VMEM((2, NZ, NX, QMSG, 128), BF16),
            pltpu.VMEM((4, QROWS, LAT + 128), BF16),
            pltpu.VMEM((2, QROWS, CTX), F32),
            pltpu.VMEM((2, QROWS, CTX), BF16),
            pltpu.VMEM((4, QROWS, LAT), F32),
            pltpu.VMEM((4, QROWS, 128), F32),
            pltpu.VMEM((4, QROWS, 128), F32),
            pltpu.VMEM((32, LAT + ROPE), F32),
            pltpu.VMEM((rows, LAT), F32),
            pltpu.VMEM((rows, 128), F32),
            pltpu.VMEM((rows, 128), F32),
            pltpu.VMEM((2, NSEQ, PMSG, 128), BF16),
            pltpu.VMEM((2, NSEQ, PMSG, 128), BF16),
            pltpu.SemaphoreType.DMA((9,)),
            pltpu.SemaphoreType.DMA((9,)),
            pltpu.SemaphoreType.DMA((10,)),
            pltpu.SemaphoreType.DMA((2, 12)),
            pltpu.SemaphoreType.DMA((2, 12)),
            pltpu.SemaphoreType.DMA((2, 6)),
            pltpu.SemaphoreType.DMA((2, 6)),
            pltpu.SemaphoreType.DMA((2, NSEQ)),
            pltpu.SemaphoreType.DMA((2, NSEQ)),
        ],
        compiler_params=pltpu.CompilerParams(
            collective_id=0, has_side_effects=True, vmem_limit_bytes=56 * 1024 * 1024
        ),
        name="latent_attention",
    )(
        q_nope.reshape(rows, 128),
        q_rope.reshape(rows, ROPE),
        w_absorb,
        w_value,
        cache.transpose(0, 2, 1),
        res_len,
        prefill_rows.transpose(0, 1, 3, 2),
        block_dest,
        new_rows.transpose(1, 0, 2),
    )
    return out.reshape(q_nope.shape)


def solution(mesh):
    in_specs = (
        P("group", None, "seq", None),
        P("group", None, "seq", None),
        P("seq", None, None),
        P("seq", None, None),
        P("group", "seq", None),
        P("group"),
        P("group", "seq", None, None),
        P("group", "seq"),
        P("group", None, None),
    )
    out_specs = P("group", None, "seq", None)
    return jax.shard_map(body, mesh=mesh, in_specs=in_specs, out_specs=out_specs, check_vma=False)
```

```python
import functools
import math

import jax
import jax.numpy as jnp
from jax import lax
from jax.experimental import pallas as pl
from jax.experimental.pallas import tpu as pltpu
from jax.sharding import PartitionSpec as P

MESH = pl.DeviceIdType.MESH
F32 = jnp.float32
BF16 = jnp.bfloat16

NY, NC, NZ, NX = 4, 2, 4, 4
HEADS = 8
STEPS = 3
PART = STEPS * HEADS
ROWS = 2 * PART
NSEQ = NZ * NX
QROWS = NSEQ * PART
LAT, ROPE = 512, 64
BLK = 128
CTX = 2048
QMSG = 4 * ROWS + 32
QCUT = QMSG // 2
PMSG = 4 * ROWS + 16
ROW = LAT + ROPE
KMSG = 16 + 2 * ROW
NEG = -1e30
EXPC = (128 + 64) ** -0.5 * math.log2(math.e)

ALONG_Y = (1, 3, 2)
FAR_FIRST = [
    (1, 2), (2, 1), (3, 2), (2, 3), (2, 2), (1, 1), (3, 3), (1, 3), (3, 1), (0, 2), (2, 0), (0, 1), (1, 0), (0, 3), (3, 0),
]


def dot_t(a, b):
    return lax.dot_general(a, b, (((1,), (1,)), ((), ())), preferred_element_type=F32)


def dot(a, b):
    return jnp.dot(a, b, preferred_element_type=F32)


def kernel(
    qn_hbm, qr_hbm, wa_hbm, wv_hbm, cache_hbm, len_hbm, pre_hbm, dest_hbm, new_hbm,
    out_ref,
    qn_ref, qr_ref, len_ref, dest_ref, new_ref, wa, wv, cache, pre, ysend, kv, qbuf, qall, scores, weights, acc, peak, total,
    fresh, fresh_w, fresh_m, fresh_l, pout, pin,
    local_sem, y_ss, y_rs, a_ss, a_rs, f_ss, f_rs, p_ss, p_rs,
):
    g, s = lax.axis_index("group"), lax.axis_index("seq")
    y, c = lax.div(g, NC), lax.rem(g, NC)
    z, x = lax.div(s, NX), lax.rem(s, NX)

    def group_dev(dy, core):
        return (lax.rem(y + dy, NY) * NC + core, s)

    def seq_dev(dz, dx):
        return (g, lax.rem(z + dz, NZ) * NX + lax.rem(x + dx, NX))

    loads = [
        pltpu.make_async_copy(src, dst, local_sem.at[i])
        for i, (src, dst) in enumerate(
            [
                (dest_hbm, dest_ref), (pre_hbm.at[0], pre), (qn_hbm, qn_ref), (qr_hbm, qr_ref), (wa_hbm, wa),
                (new_hbm, new_ref), (len_hbm, len_ref), (cache_hbm, cache), (wv_hbm, wv),
            ]
        )
    ]
    barrier = pltpu.get_barrier_semaphore()
    for device in (
        [group_dev(dy, core) for dy in ALONG_Y for core in range(NC)]
        + [group_dev(0, 1 - c)]
        + [seq_dev(0, d) for d in (1, 2, 3)]
        + [seq_dev(d, 0) for d in (1, 2, 3)]
    ):
        pl.semaphore_signal(barrier, inc=1, device_id=device, device_id_type=MESH)

    for load in loads:
        load.start()

    def start(copies):
        for copy in copies:
            copy.start()
        return copies

    loads[0].wait()
    owners = [dest_ref[0, k] for k in range(8)]
    targets = [lax.div(o, 2) for o in owners]
    members = [lax.rem(o, 2) for o in owners]
    tag_row = lax.broadcasted_iota(jnp.int32, (16, 128), 0)

    def pick(to, wanted):
        first = second = jnp.int32(0)
        tag_first = tag_second = jnp.int32(2)
        for k in reversed(range(8)):
            match = targets[k] == wanted
            second = jnp.where(match, first, second)
            tag_second = jnp.where(match, tag_first, tag_second)
            first = jnp.where(match, k, first)
            tag_first = jnp.where(match, members[k], tag_first)
        for slot, index in enumerate((first, second)):
            to[pl.ds(16 + slot * ROW, ROW), :] = pre[index]
        tags = jnp.where(tag_row < 8, tag_first, tag_second)
        to[pl.ds(0, 16), :] = tags.astype(F32).astype(BF16)

    def core_copy():
        return pltpu.make_async_remote_copy(
            src_ref=ysend.at[6], dst_ref=kv.at[1], send_sem=y_ss.at[6], recv_sem=y_rs.at[1],
            device_id=group_dev(0, 1 - c), device_id_type=MESH,
        )

    parts = [pl.ds(0, KMSG), pl.ds(0, 16 + ROW), pl.ds(16 + ROW, ROW)]

    def y_copy(k, core, part):
        there = 2 + 2 * ALONG_Y.index((NY - ALONG_Y[k]) % NY) + c
        late = 2 if part == 2 else 0
        return pltpu.make_async_remote_copy(
            src_ref=ysend.at[3 * core + k, parts[part]], dst_ref=kv.at[there, parts[part]],
            send_sem=y_ss.at[3 * core + k + (5 - 2 * core if late else 0)], recv_sem=y_rs.at[there + late],
            device_id=group_dev(ALONG_Y[k], core), device_id_type=MESH,
        )

    def pick_for(core):
        for k in range(3):
            pick(ysend.at[3 * core + k], lax.rem(y + ALONG_Y[k], NY) * NC + core)

    def blocks_to(core):
        return start(
            [y_copy(k, core, part) for k in range(3) for part in (0,)]
        )

    loads[1].wait()
    pick_for(1)

    pl.semaphore_wait(barrier, 2 * NY - 1 + 6)
    group_copies = blocks_to(1)

    for load in loads[2:5]:
        load.wait()
    row = lax.broadcasted_iota(jnp.int32, (2 * ROWS, 128), 0)
    own = qn_ref[...].astype(F32)
    spread = [jnp.where((row & 7) == h, own, 0.0).astype(BF16) for h in range(HEADS)]
    q_latent = dot(jnp.concatenate(spread, axis=1), wa[...].reshape(HEADS * 128, LAT))
    q_latent = q_latent.astype(BF16)
    for pair in range(2):
        rows = slice(pair * ROWS, (pair + 1) * ROWS)
        for p in range(4):
            qbuf[pair, 0, 0, pl.ds(p * ROWS, ROWS), :] = q_latent[rows, p * 128 : (p + 1) * 128]
        ropes = [qr_ref[pl.ds(pair * ROWS + 16 * i, 16), :] for i in range(3)]
        ropes.append(jnp.zeros((16, ROPE), BF16))
        for i in range(2):
            qbuf[pair, 0, 0, pl.ds(4 * ROWS + 16 * i, 16), :] = jnp.concatenate(
                ropes[2 * i : 2 * i + 2], axis=1
            )

    low, high = pl.ds(0, QCUT), pl.ds(QCUT, QMSG - QCUT)

    def own_copy(pair, index, dz, dx, rows):
        return pltpu.make_async_remote_copy(
            src_ref=qbuf.at[pair, 0, 0, rows], dst_ref=qbuf.at[pair, (NZ - dz) % NZ, (NX - dx) % NX, rows],
            send_sem=a_ss.at[pair, index], recv_sem=a_rs.at[pair, index],
            device_id=seq_dev(dz, dx), device_id_type=MESH,
        )

    def x_first(pair):
        return [own_copy(pair, d - 1, 0, d, low) for d in (1, 2, 3)]

    def z_first(pair):
        return [own_copy(pair, 2 + d, d, 0, high) for d in (1, 2, 3)]

    def rest(pair):
        return [own_copy(pair, 5 + d, 0, d, high) for d in (1, 2, 3)] + [
            own_copy(pair, 8 + d, d, 0, low) for d in (1, 2, 3)
        ]

    def forward_z(pair):
        return [
            pltpu.make_async_remote_copy(
                src_ref=qbuf.at[pair, 0, pl.ds(1, 3), low], dst_ref=qbuf.at[pair, NZ - d, pl.ds(1, 3), low],
                send_sem=f_ss.at[pair, d - 1], recv_sem=f_rs.at[pair, d - 1],
                device_id=seq_dev(d, 0), device_id_type=MESH,
            )
            for d in (1, 2, 3)
        ]

    def forward_x(pair):
        return [
            pltpu.make_async_remote_copy(
                src_ref=qbuf.at[pair, pl.ds(1, 3), 0, high], dst_ref=qbuf.at[pair, pl.ds(1, 3), NX - d, high],
                send_sem=f_ss.at[pair, 2 + d], recv_sem=f_rs.at[pair, 2 + d],
                device_id=seq_dev(0, d), device_id_type=MESH,
            )
            for d in (1, 2, 3)
        ]

    def arrived(copies):
        for copy in copies:
            copy.wait_recv()

    first_x, first_z = start(x_first(0)), start(z_first(0))
    others = start(rest(0))
    first_x1, first_z1 = start(x_first(1)), start(z_first(1))
    arrived(first_x)
    forward_z0 = start(forward_z(0))
    arrived(first_z)
    forward_x0 = start(forward_x(0))
    others1 = start(rest(1))
    sent = first_x + first_z + others + first_x1 + first_z1 + others1
    arrived(first_x1)
    forward_z1 = start(forward_z(1))
    arrived(first_z1)
    forward_x1 = start(forward_x(1))
    sent += forward_z0 + forward_x0 + forward_z1 + forward_x1

    pick_for(0)
    group_copies += blocks_to(0)
    pick(ysend.at[6], y * NC + 1 - c)
    group_copies += start([core_copy()])
    pick(kv.at[0], y * NC + c)

    loads[5].wait()
    fresh[...] = jnp.zeros_like(fresh)
    for u in range(STEPS):
        new = new_ref[u].astype(F32)
        for r in range(4):
            fresh[pl.ds(8 * r + u, 1), :] = new[r : r + 1]
    fresh_rows = fresh[...].astype(BF16)
    s_fresh = dot_t(q_latent, fresh_rows[:, :LAT]) + dot_t(
        qr_ref[...], fresh_rows[:, LAT : LAT + ROPE]
    )
    part = lax.broadcasted_iota(jnp.int32, (2 * ROWS, 32), 0) >> 3
    key = lax.broadcasted_iota(jnp.int32, (2 * ROWS, 32), 1)
    request = (
        (part >= 3).astype(jnp.int32) + (part >= 6).astype(jnp.int32) + (part >= 9).astype(jnp.int32)
    )
    step = part - 3 * request
    allowed = ((key >> 3) == request) & ((key & 7) <= step)
    s_fresh = jnp.where(allowed, s_fresh, NEG)
    m_fresh = jnp.max(s_fresh, axis=1, keepdims=True)
    p_fresh = jnp.where(allowed, jnp.exp2((s_fresh - m_fresh) * EXPC), 0.0)
    fresh_m[...] = jnp.broadcast_to(m_fresh, fresh_m.shape)
    fresh_l[...] = jnp.broadcast_to(jnp.sum(p_fresh, axis=1, keepdims=True), fresh_l.shape)
    fresh_w[...] = dot(p_fresh.astype(BF16), fresh_rows[:, :LAT])

    def assemble(pair):
        def two(i, carry):
            at = pl.multiple_of(i * 2 * PART, 16)
            dz, dx = lax.div(i, 2), lax.rem(i, 2) * 2
            def part(d, p):
                if p < 4:
                    return qbuf[pair, dz, dx + d, pl.ds(p * ROWS, ROWS), :].astype(F32)
                first, second = (
                    qbuf[pair, dz, dx + d, pl.ds(4 * ROWS + 16 * i, 16), :].astype(F32) for i in range(2)
                )
                return jnp.concatenate([first, pltpu.roll(first, ROPE, 1), second], axis=0)

            for p in range(5):
                one, two = part(0, p), part(1, p)
                lanes = slice(p * 128, (p + 1) * 128)
                for r in range(2):
                    rows = slice(r * PART, (r + 1) * PART)
                    qall[2 * pair + r, pl.ds(at, 2 * PART), lanes] = jnp.concatenate(
                        [one[rows], two[rows]], axis=0
                    ).astype(BF16)
            return carry

        lax.fori_loop(0, NSEQ // 2, two, 0)

    def partial_copy(pair, j):
        dz, dx = lax.div(j, NX), lax.rem(j, NX)
        there = lax.rem(NZ - dz, NZ) * NX + lax.rem(NX - dx, NX)
        return pltpu.make_async_remote_copy(
            src_ref=pout.at[pair, j], dst_ref=pin.at[pair, there],
            send_sem=p_ss.at[pair, j], recv_sem=p_rs.at[pair, there],
            device_id=seq_dev(dz, dx), device_id_type=MESH,
        )

    def message(pair, j, lane, sums, peaks, totals):
        for p in range(4):
            lanes = slice(p * 128, (p + 1) * 128)
            pout[pair, j, pl.ds(p * ROWS, ROWS), :] = jnp.concatenate(
                [part[:, lanes] for part in sums], axis=0
            ).astype(BF16)
        m, l = jnp.concatenate(peaks, axis=0), jnp.concatenate(totals, axis=0)
        m_high = m.astype(BF16).astype(F32)
        m_mid = (m - m_high).astype(BF16).astype(F32)
        m_low = m - m_high - m_mid
        l_high = l.astype(BF16).astype(F32)
        stats = jnp.zeros((16, 128), F32)
        for i in range(3):
            rows = slice(16 * i, 16 * (i + 1))
            for q, value in enumerate((m_high, m_mid, m_low, l_high, l - l_high)):
                stats = jnp.where(lane == 8 * i + q, value[rows], stats)
        pout[pair, j, pl.ds(4 * ROWS, 16), :] = stats.astype(BF16)

    def pack(pair):
        lane = lax.broadcasted_iota(jnp.int32, (16, 128), 1)

        def one(j, carry):
            rows = pl.ds(j * PART, PART)
            message(
                pair, j, lane, *([ref[2 * pair + r, rows, :] for r in range(2)] for ref in (acc, peak, total))
            )
            return carry

        for dz, dx in FAR_FIRST + [(0, 0)]:
            one(dz * NX + dx, 0)
            if dz or dx:
                partial_copy(pair, dz * NX + dx).start()

    def partial_copies(pair):
        return [partial_copy(pair, dz * NX + dx) for dz, dx in FAR_FIRST]

    def finish(pair):
        stats = jnp.concatenate(
            [pout[pair, 0, pl.ds(4 * ROWS, 16), :]]
            + [pin[pair, j, pl.ds(4 * ROWS, 16), :] for j in range(1, NSEQ)],
            axis=0,
        )
        source = lax.broadcasted_iota(jnp.int32, (128, 128), 0)
        picks = [
            ((source >= 8 * i) & (source < 8 * i + 3)).astype(F32).astype(BF16) for i in range(3)
        ] + [
            ((source >= 8 * i + 3) & (source < 8 * i + 5)).astype(F32).astype(BF16) for i in range(3)
        ]
        spread_stats = dot(stats, jnp.concatenate(picks, axis=1))

        def of(j, kind):
            return jnp.concatenate(
                [
                    spread_stats[16 * j : 16 * (j + 1), 128 * (3 * kind + i) : 128 * (3 * kind + i + 1)]
                    for i in range(3)
                ],
                axis=0,
            )

        rows = pl.ds(pair * ROWS, ROWS)
        peaks = [of(j, 0) for j in range(NSEQ)]
        m_fresh = fresh_m[rows, :]
        top = m_fresh
        for m in peaks:
            top = jnp.maximum(top, m)
        keep = jnp.exp2((m_fresh - top) * EXPC)
        sums = keep * fresh_l[rows, :]
        values = [keep * fresh_w[rows, p * 128 : (p + 1) * 128] for p in range(4)]
        for j in range(NSEQ):
            keep = jnp.exp2((peaks[j] - top) * EXPC)
            sums = sums + keep * of(j, 1)
            message = pout if j == 0 else pin
            for p in range(4):
                values[p] = values[p] + keep * message[pair, j, pl.ds(p * ROWS, ROWS), :].astype(F32)
        head = lax.broadcasted_iota(jnp.int32, (ROWS, 128), 0) & 7
        attended = [(v / sums).astype(BF16).astype(F32) for v in values]
        spread = [
            jnp.where(head == h, attended[p], 0.0).astype(BF16) for h in range(HEADS) for p in range(4)
        ]
        result = dot(jnp.concatenate(spread, axis=1), wv[...].reshape(HEADS * LAT, 128))
        out_ref[rows, :] = result.astype(BF16)

    arrived(others + forward_z0 + forward_x0)
    assemble(0)
    loads[6].wait()
    loads[7].wait()

    tile = 512
    tiles = range(CTX // tile)
    position = lax.broadcasted_iota(jnp.int32, (QROWS, tile), 1)

    def score(r, k, running):
        keys = pl.ds(k * tile, tile)
        sc = dot(qall[r, :, :ROW], cache[r, :, keys])
        sc = jnp.where(position < len_ref[r] - s * CTX - k * tile, sc, NEG)
        scores[r, :, keys] = sc
        for i in range(tile // 128):
            running = jnp.maximum(running, sc[:, i * 128 : (i + 1) * 128])
        return running

    def weigh(r, k, m, sums):
        keys = pl.ds(k * tile, tile)
        w = jnp.exp2((scores[r, :, keys] - m) * EXPC)
        for i in range(tile // 128):
            sums = sums + w[:, i * 128 : (i + 1) * 128]
        weights[r, :, keys] = w.astype(BF16)
        return sums

    def done(r, m, sums):
        peak[r] = jnp.broadcast_to(m, (QROWS, 128))
        total[r] = jnp.broadcast_to(jnp.sum(sums, axis=1, keepdims=True), (QROWS, 128))

    lowest, nothing = jnp.full((QROWS, 128), NEG, F32), jnp.zeros((QROWS, 128), F32)
    m0 = m1 = lowest
    for k in tiles:
        m0 = score(0, k, m0)
    m0 = jnp.max(m0, axis=1, keepdims=True)
    sums0 = sums1 = nothing
    for k in tiles:
        m1 = score(1, k, m1)
        sums0 = weigh(0, k, m0, sums0)
    m1 = jnp.max(m1, axis=1, keepdims=True)
    done(0, m0, sums0)
    acc[0] = dot_t(weights[0], cache[0, :LAT, :])
    for k in tiles:
        sums1 = weigh(1, k, m1, sums1)
    done(1, m1, sums1)
    acc[1] = dot_t(weights[1], cache[1, :LAT, :])
    pack(0)
    partials0 = partial_copies(0)

    arrived(others1 + forward_z1 + forward_x1)
    assemble(1)
    for r in (2, 3):
        acc[r] = jnp.zeros((QROWS, LAT), F32)
        peak[r] = jnp.full((QROWS, 128), NEG, F32)
        total[r] = jnp.zeros((QROWS, 128), F32)

    def blocks(taken, last=False):
        keys = jnp.concatenate([kv[i, pl.ds(16 + slot * ROW, ROW), :] for i, slot in taken], axis=1)
        tag = jnp.concatenate(
            [kv[i, pl.ds(0, 16), :].astype(F32)[8 * slot : 8 * slot + 1] for i, slot in taken], axis=1
        )
        count = len(taken)
        new = (2, 3)
        scs = [jnp.where(tag == float(r - 2), dot(qall[r, :, :ROW], keys), NEG) for r in new]
        pieces = [[sc[:, n * 128 : (n + 1) * 128] for n in range(count)] for sc in scs]
        olds = [peak[r] for r in new]
        tops = [
            jnp.maximum(old, jnp.max(functools.reduce(jnp.maximum, some), axis=1, keepdims=True))
            for old, some in zip(olds, pieces)
        ]
        ws = [[jnp.exp2((piece - top) * EXPC) for piece in some] for some, top in zip(pieces, tops)]
        terms = [dot_t(jnp.concatenate(w, axis=1).astype(BF16), keys[:LAT]) for w in ws]
        keeps = [jnp.exp2((old - top) * EXPC) for old, top in zip(olds, tops)]
        totals = [
            total[r] * keep + jnp.sum(sum(w[1:], w[0]), axis=1, keepdims=True)
            for r, keep, w in zip(new, keeps, ws)
        ]
        four = [slice(p * 128, (p + 1) * 128) for p in range(4)]
        if last:
            lane = lax.broadcasted_iota(jnp.int32, (16, 128), 1)
            for dz, dx in FAR_FIRST + [(0, 0)]:
                j = dz * NX + dx
                rows = slice(j * PART, (j + 1) * PART)
                sums = [
                    jnp.concatenate(
                        [acc[r, rows, lanes] * keep[rows] + term[rows, lanes] for lanes in four], axis=1
                    )
                    for r, keep, term in zip(new, keeps, terms)
                ]
                message(1, j, lane, sums, [top[rows] for top in tops], [t[rows] for t in totals])
                if j > 0:
                    partial_copy(1, j).start()
            return
        for r, keep, top, sums, term in zip(new, keeps, tops, totals, terms):
            peak[r] = top
            total[r] = sums
            for lanes in four:
                acc[r, :, lanes] = acc[r, :, lanes] * keep + term[:, lanes]

    def landed(i, part, sem):
        pltpu.make_async_remote_copy(
            src_ref=ysend.at[6, parts[part]], dst_ref=kv.at[i, parts[part]],
            send_sem=y_ss.at[6], recv_sem=y_rs.at[sem],
            device_id=group_dev(0, 1 - c), device_id_type=MESH,
        ).wait_recv()

    landed(1, 0, 1)

    def four(k, carry):
        @pl.when(k > 0)
        def _():
            landed(2 * k, 0, 2 * k)
            landed(2 * k + 1, 0, 2 * k + 1)

        blocks([(2 * k, 0), (2 * k, 1), (2 * k + 1, 0), (2 * k + 1, 1)])
        return carry

    lax.fori_loop(0, 3, four, 0)
    landed(6, 0, 6)
    landed(7, 0, 7)
    blocks([(6, 0), (6, 1), (7, 0), (7, 1)], last=True)
    partials1 = partial_copies(1)
    loads[8].wait()
    arrived(partials0)
    finish(0)
    arrived(partials1)
    finish(1)
    for copy in group_copies + sent + partials0 + partials1:
        copy.wait_send()


def body(q_nope, q_rope, w_absorb, w_value, cache, res_len, prefill_rows, block_dest, new_rows):
    rows = 4 * PART
    out = pl.pallas_call(
        kernel,
        out_shape=jax.ShapeDtypeStruct((rows, 128), BF16),
        in_specs=[pl.BlockSpec(memory_space=pl.ANY)] * 9,
        out_specs=pl.BlockSpec(memory_space=pltpu.VMEM),
        scratch_shapes=[
            pltpu.VMEM((rows, 128), BF16),
            pltpu.VMEM((rows, ROPE), BF16),
            pltpu.SMEM(res_len.shape, jnp.int32),
            pltpu.SMEM(block_dest.shape, jnp.int32),
            pltpu.VMEM((STEPS, 4, ROW), BF16),
            pltpu.VMEM(w_absorb.shape, BF16),
            pltpu.VMEM(w_value.shape, BF16),
            pltpu.VMEM((2, ROW, CTX), BF16),
            pltpu.VMEM((8, ROW, BLK), BF16),
            pltpu.VMEM((7, KMSG, 128), BF16),
            pltpu.VMEM((8, KMSG, 128), BF16),
            pltpu.VMEM((2, NZ, NX, QMSG, 128), BF16),
            pltpu.VMEM((4, QROWS, LAT + 128), BF16),
            pltpu.VMEM((2, QROWS, CTX), F32),
            pltpu.VMEM((2, QROWS, CTX), BF16),
            pltpu.VMEM((4, QROWS, LAT), F32),
            pltpu.VMEM((4, QROWS, 128), F32),
            pltpu.VMEM((4, QROWS, 128), F32),
            pltpu.VMEM((32, LAT + ROPE), F32),
            pltpu.VMEM((rows, LAT), F32),
            pltpu.VMEM((rows, 128), F32),
            pltpu.VMEM((rows, 128), F32),
            pltpu.VMEM((2, NSEQ, PMSG, 128), BF16),
            pltpu.VMEM((2, NSEQ, PMSG, 128), BF16),
            pltpu.SemaphoreType.DMA((9,)),
            pltpu.SemaphoreType.DMA((9,)),
            pltpu.SemaphoreType.DMA((10,)),
            pltpu.SemaphoreType.DMA((2, 12)),
            pltpu.SemaphoreType.DMA((2, 12)),
            pltpu.SemaphoreType.DMA((2, 6)),
            pltpu.SemaphoreType.DMA((2, 6)),
            pltpu.SemaphoreType.DMA((2, NSEQ)),
            pltpu.SemaphoreType.DMA((2, NSEQ)),
        ],
        compiler_params=pltpu.CompilerParams(
            collective_id=0, has_side_effects=True, vmem_limit_bytes=56 * 1024 * 1024
        ),
        name="latent_attention",
    )(
        q_nope.reshape(rows, 128),
        q_rope.reshape(rows, ROPE),
        w_absorb,
        w_value,
        cache.transpose(0, 2, 1),
        res_len,
        prefill_rows.transpose(0, 1, 3, 2),
        block_dest,
        new_rows.transpose(1, 0, 2),
    )
    return out.reshape(q_nope.shape)


def solution(mesh):
    in_specs = (
        P("group", None, "seq", None),
        P("group", None, "seq", None),
        P("seq", None, None),
        P("seq", None, None),
        P("group", "seq", None),
        P("group"),
        P("group", "seq", None, None),
        P("group", "seq"),
        P("group", None, None),
    )
    out_specs = P("group", None, "seq", None)
    return jax.shard_map(body, mesh=mesh, in_specs=in_specs, out_specs=out_specs, check_vma=False)
```
